32 devices in a mesh: grp: 2 (over y), seq: 4 (over z), sub: 2 (over x), rep: 2 (over core).
Axes of the slice: x: 2, y: 2, z: 4, core: 2. Of those that a mesh axis runs over, the one named last changes fastest.
Arguments:
- inputs: bfloat16 [16, 4096, 4096], P(('grp', 'rep'), ('seq', 'sub')), parts along dimension 0, may hold values from -6 to 6
- out_grads: bfloat16 [16, 4096, 4096], P(('grp', 'rep'), ('seq', 'sub')), parts along dimension 0, may hold values from -6 to 6
- doc_lengths: int32 [16], P(('grp', 'rep')), parts along dimension 0, may hold values from 512 to 4096, as said below
- in_proj: bfloat16 [4096, 256], replicated, may hold values from -0.09375 to 0.09375
- out_proj: bfloat16 [4096, 256], replicated, may hold values from -0.09375 to 0.09375
- in_factor: float32 [256, 256], replicated, may hold values from -0.25 to 2.25, as said below
- out_factor: float32 [256, 256], replicated, may hold values from -0.25 to 2.25, as said below
- index_rows: bfloat16 [4096, 65536], P('grp', ('seq', 'sub', 'rep')), parts along dimension 0, may hold values from -0.00048828125 to 0.00048828125
Outputs:
- scores: float32 [4096, 8], P(('grp', 'seq', 'sub', 'rep')), parts along dimension 0
The draws below stay inside these ranges and needn't reach their ends.
There are 2 independent parts, one for each index of `grp`. The reference program is written for one: setup_inputs(seed, part) draws one part's arguments, and reference() takes and returns one part's arrays. A program takes and returns all parts, laid end to end along the dimension named above; an argument that names none is the same for every part. Nothing has to cross between parts.
Inputs may be any that keep to these rules, and one draw needn't show every extreme that they name: `doc_lengths`: positions from a document's length on are padding. `in_factor`: symmetric. `out_factor`: symmetric.
All inputs are finite; a program needn't handle non-finite values.
Results may differ from the reference program's by a relative error of at most 0.005.
Values may be sent and summed in bfloat16 or wider, within the bound.
A program may use at most 128 MiB of HBM per device.

```python
import jax
import jax.numpy as jnp
from jax import lax

D = 4096
R = 256
LEN = 4096
DOCS = 8
ROWS = 2048
F = 65536


def factor_matrix(key):
    key_diag, key_noise = jax.random.split(key)
    diagonal_part = jax.random.uniform(key_diag, (R,), jnp.float32, 0.5, 2.0)
    noise = jax.random.normal(key_noise, (R, R), jnp.float32)
    noise = jnp.clip(noise, -4.0, 4.0)
    symmetric = (noise + noise.T) * (0.25 / jnp.sqrt(jnp.float32(R)))
    return (jnp.diag(diagonal_part) + symmetric).astype(jnp.float32)


def draw_in_factor(key, part):
    return factor_matrix(jax.random.fold_in(key, 11))


def draw_out_factor(key, part):
    return factor_matrix(jax.random.fold_in(key, 23))


def draw_doc_lengths(key, part):
    key_len, key_perm = jax.random.split(jax.random.fold_in(key, 37))
    lengths = jax.random.randint(key_len, (DOCS,), LEN // 8, LEN + 1).astype(jnp.int32)
    order = jax.random.permutation(key_perm, DOCS)
    lengths = lengths.at[order[0]].set(LEN)
    lengths = lengths.at[order[1]].set(LEN // 8)
    return lengths.astype(jnp.int32)


def raised(drawn, stream_key, source, target, parts, factor):
    def block_of(position):
        return (jnp.arange(drawn.shape[position]) // (drawn.shape[position] // parts)).reshape((-1,) + (1,) * (drawn.ndim - 1 - position))

    first = jax.random.permutation(stream_key, parts)[block_of(target)]
    other_side = (block_of(target) + parts // 2) % parts
    return jnp.where((block_of(source) == first) | (block_of(source) == other_side), factor * drawn, drawn)


def level_of(own_key, dims, cuts, low, largest):
    gain = 1.0
    for position, parts in cuts:
        draws = jax.random.uniform(jax.random.fold_in(jax.random.fold_in(own_key, 6), position), (parts,), jnp.float32, low / len(cuts), largest / len(cuts))
        gain = gain * jnp.repeat(jnp.exp(draws), dims[position] // parts).reshape((-1,) + (1,) * (len(dims) - 1 - position))
    return gain


def centred(key, dims, deviation, bound, shards=(), kind=jnp.bfloat16):
    array = jax.random.normal(key, dims, jnp.float32) * deviation
    if len(shards) > 0:
        array = level_of(key, dims, shards, -0.22, 0.18) * array
    return jnp.clip(array, min=-bound, max=bound).astype(kind)


def heavy_noise(own_key, dims, deviation, reach, cuts, heavy, held_as=jnp.bfloat16):
    drawn = deviation * jax.random.normal(own_key, dims, jnp.float32)
    if cuts:
        drawn = drawn * level_of(own_key, dims, cuts, -0.22, 0.18)
    return jnp.clip(raised(drawn, jax.random.fold_in(own_key, 3), *heavy), -reach, reach).astype(held_as)


def setup_inputs(seed: int = 0, part: int = 0) -> dict:
    key_list = jax.random.split(jax.random.key(seed), 9)
    part_keys = jax.random.split(jax.random.fold_in(key_list[8], part), 9)
    inputs = centred(part_keys[0], (DOCS, LEN, D), 1.0, 6.0, ((0, 2), (1, 8)))
    out_grads = centred(part_keys[1], (DOCS, LEN, D), 1.0, 6.0, ((0, 2), (1, 8)))
    doc_lengths = draw_doc_lengths(jax.random.fold_in(jax.random.fold_in(key_list[8], part), 71), part)
    in_proj = centred(key_list[3], (D, R), D ** -0.5, 0.09375)
    out_proj = centred(key_list[4], (D, R), D ** -0.5, 0.09375)
    in_factor = draw_in_factor(jax.random.fold_in(key_list[8], 71), part)
    out_factor = draw_out_factor(jax.random.fold_in(key_list[8], 71), part)
    index_rows = heavy_noise(part_keys[7], (ROWS, F), (F * LEN) ** -0.5, 0.00048828125, ((1, 16),), (1, 0, 16, 2.0))
    return {"inputs": inputs, "out_grads": out_grads, "doc_lengths": doc_lengths, "in_proj": in_proj, "out_proj": out_proj, "in_factor": in_factor, "out_factor": out_factor, "index_rows": index_rows}


def reference(inputs, out_grads, doc_lengths, in_proj, out_proj, in_factor, out_factor, index_rows):
    positions = jnp.arange(LEN, dtype=jnp.int32)

    def per_document(operands):
        act_rows, grad_rows, length = operands
        in_rows = jnp.dot(act_rows, in_proj, preferred_element_type=jnp.float32).astype(jnp.bfloat16)
        out_rows = jnp.dot(grad_rows, out_proj, preferred_element_type=jnp.float32).astype(jnp.bfloat16)
        live = (positions < length).astype(jnp.bfloat16)
        masked = out_rows * live[:, None]
        grad = jnp.dot(masked.T, in_rows, preferred_element_type=jnp.float32)
        left = jnp.dot(out_factor, grad, precision=lax.Precision.HIGHEST)
        precond = jnp.dot(left, in_factor, precision=lax.Precision.HIGHEST)
        return precond.reshape(-1).astype(jnp.bfloat16)

    precond = lax.map(per_document, (inputs, out_grads, doc_lengths))
    return jnp.dot(index_rows, precond.T, preferred_element_type=jnp.float32)
```

```python
import functools

import jax
import jax.numpy as jnp
from jax import lax
from jax.experimental import pallas as pl
from jax.experimental.pallas import tpu as pltpu
from jax.sharding import PartitionSpec as P

MESH = pl.DeviceIdType.MESH
F32 = jnp.float32
BF16 = jnp.bfloat16
OWNERS = ("seq", "sub", "rep")
PIECES = 4
SLOTS = 8


def two_parts(x):
    high = x.astype(BF16)
    return high, (x - high.astype(F32)).astype(BF16)


def dot3(a, b):
    a_high, a_low = two_parts(a)
    b_high, b_low = two_parts(b)
    small = jnp.dot(a_high, b_low, preferred_element_type=F32) + jnp.dot(
        a_low, b_high, preferred_element_type=F32
    )
    return jnp.dot(a_high, b_high, preferred_element_type=F32) + small


def kernel(
    sizes,
    x_hbm, g_hbm, len_ref, wi_hbm, wo_hbm, fi_hbm, fo_hbm, idx_hbm,
    out_ref,
    xbuf, idxbuf, wi, wo, fi, fo, in_rows, out_rows, send, recv, summed, sc_send, sc_recv,
    piece_sem, idx_sem, weight_sem, send_sem, recv_sem, sc_send_sem, sc_recv_sem,
):
    n_seq, n_sub, n_rep = sizes
    n = n_seq * n_sub * n_rep
    docs, tok, _ = x_hbm.shape
    half = tok // 2
    blocks = n // n_rep
    rows = idx_hbm.shape[0] // blocks
    lanes = rows // n_rep
    place = lax.axis_index("seq") * n_sub + lax.axis_index("sub")
    my_rep = lax.axis_index("rep")
    me = place * n_rep + my_rep

    def device(p):
        return {
            "seq": lax.div(p, n_sub * n_rep),
            "sub": lax.rem(lax.div(p, n_rep), n_sub),
            "rep": lax.rem(p, n_rep),
        }

    def piece_copy(d, q):
        source = x_hbm if q < 2 else g_hbm
        slot = lax.rem(d, SLOTS // PIECES) * PIECES + q
        return pltpu.make_async_copy(
            source.at[d, pl.ds((q % 2) * half, half), :], xbuf.at[slot], piece_sem.at[slot]
        )

    def block_at(t):
        return lax.rem(place + 1 + t, blocks)

    def idx_copy(t):
        c = block_at(t)
        return pltpu.make_async_copy(
            idx_hbm.at[pl.ds(c * rows, rows), :], idxbuf.at[t], idx_sem.at[t]
        )

    def weight_copy(k):
        source, target = ((wi_hbm, wi), (wo_hbm, wo), (fo_hbm, fo), (fi_hbm, fi))[k]
        return pltpu.make_async_copy(source, target, weight_sem.at[k])

    def doc_copy(d, source, p):
        return pltpu.make_async_remote_copy(
            src_ref=send.at[d, p],
            dst_ref=recv.at[source, d],
            send_sem=send_sem.at[d, p],
            recv_sem=recv_sem.at[source, d],
            device_id=device(p),
            device_id_type=MESH,
        )

    def score_copy(source, p):
        return pltpu.make_async_remote_copy(
            src_ref=sc_send.at[p],
            dst_ref=sc_recv.at[source],
            send_sem=sc_send_sem.at[p],
            recv_sem=sc_recv_sem.at[source],
            device_id=device(p),
            device_id_type=MESH,
        )

    weight_copy(0).start()
    piece_copy(0, 0).start()
    piece_copy(0, 1).start()
    weight_copy(1).start()
    piece_copy(0, 2).start()
    piece_copy(0, 3).start()
    weight_copy(2).start()
    weight_copy(3).start()
    for q in range(PIECES):
        piece_copy(1, q).start()

    barrier = pltpu.get_barrier_semaphore()

    def greet(s, carry):
        p = lax.rem(me + s, n)
        pl.semaphore_signal(barrier, inc=1, device_id=device(p), device_id_type=MESH)
        return carry

    lax.fori_loop(1, n, greet, 0)

    def document(d, carry):
        for q in range(PIECES):
            piece_copy(d, q).wait()
            if q % 2 == 0:

                @pl.when(d == 0)
                def _():
                    weight_copy(q // 2).wait()

            slot = lax.rem(d, SLOTS // PIECES) * PIECES + q
            part = pl.ds((q % 2) * half, half)
            w = wi if q < 2 else wo
            product = jnp.dot(xbuf[slot], w[...], preferred_element_type=F32)
            if q < 2:
                in_rows[part, :] = product.astype(BF16)
            else:
                position = (
                    place * tok + (q % 2) * half + lax.broadcasted_iota(jnp.int32, product.shape, 0)
                )
                live = position < len_ref[d]
                out_rows[part, :] = jnp.where(live, product, 0.0).astype(BF16)
            ahead = d + SLOTS // PIECES

            @pl.when(ahead < docs)
            def _():
                piece_copy(ahead, q).start()

            @pl.when(ahead >= docs)
            def _():
                idx_copy((ahead - docs) * PIECES + q).start()

        grad = lax.dot_general(
            out_rows[...], in_rows[...], (((0,), (0,)), ((), ())), preferred_element_type=F32
        )

        @pl.when(d == 0)
        def _():
            weight_copy(2).wait()
            weight_copy(3).wait()

        left = dot3(fo[...], grad)
        send[d] = left.astype(BF16).reshape(send.shape[1:])

        @pl.when(d == 0)
        def _():
            pl.semaphore_wait(barrier, n - 1)

        def push(s, c):
            doc_copy(d, me, lax.rem(me + s, n)).start()
            return c

        lax.fori_loop(1, n, push, 0)
        recv[me, d] = send[d, me]
        return carry

    lax.fori_loop(0, docs, document, 0)

    for d in range(docs):

        def arrive(s, c):
            doc_copy(d, lax.rem(me + n - s, n), lax.rem(me + s, n)).wait_recv()
            return c

        lax.fori_loop(1, n, arrive, 0)
        for r in range(n_rep):
            total = recv[r, d].astype(F32)
            for j in range(1, blocks):
                total = total + recv[j * n_rep + r, d].astype(F32)
            summed[:, r * docs + d, :] = total

    o_rows, all_docs, width = summed.shape
    precond = dot3(summed[...].reshape(o_rows * all_docs, width), fi[...])
    precond = precond.reshape(o_rows, all_docs, width)
    features = jnp.concatenate([precond[o] for o in range(o_rows)], axis=1).astype(BF16)

    def score(t, carry):
        idx_copy(t).wait()
        c = block_at(t)
        part = lax.dot_general(
            features, idxbuf[t], (((1,), (1,)), ((), ())), preferred_element_type=F32
        )
        for r in range(n_rep):
            p = c * n_rep + r
            sc_send[p] = part[:, r * lanes : (r + 1) * lanes]

            @pl.when(p != me)
            def _():
                score_copy(me, p).start()

        return carry

    lax.fori_loop(0, blocks, score, 0)
    sc_recv[me] = sc_send[me]

    def settle(s, carry):
        p = lax.rem(me + s, n)
        score_copy(lax.rem(me + n - s, n), p).wait_recv()
        return carry

    lax.fori_loop(1, n, settle, 0)
    out_ref[...] = jnp.sum(sc_recv[...], axis=0)

    def drain(s, carry):
        p = lax.rem(me + s, n)
        score_copy(me, p).wait_send()
        for d in range(docs):
            doc_copy(d, me, p).wait_send()
        return carry

    lax.fori_loop(1, n, drain, 0)


def fused(sizes, inputs, out_grads, doc_lengths, in_proj, out_proj, in_factor, out_factor, index_rows):
    n = sizes[0] * sizes[1] * sizes[2]
    docs, tok, width = inputs.shape
    rank = in_proj.shape[1]
    rows, features = index_rows.shape
    all_docs = docs * sizes[2]
    o_rows = rank // n
    blocks = n // sizes[2]
    any_ref = pl.BlockSpec(memory_space=pl.ANY)
    scores = pl.pallas_call(
        functools.partial(kernel, sizes),
        out_shape=jax.ShapeDtypeStruct((all_docs, rows // n), F32),
        in_specs=[
            any_ref, any_ref, pl.BlockSpec(memory_space=pltpu.SMEM),
            any_ref, any_ref, any_ref, any_ref, any_ref,
        ],
        out_specs=pl.BlockSpec(memory_space=pltpu.VMEM),
        scratch_shapes=[
            pltpu.VMEM((SLOTS, tok // 2, width), BF16),
            pltpu.VMEM((blocks, rows // blocks, features), BF16),
            pltpu.VMEM(in_proj.shape, BF16),
            pltpu.VMEM(out_proj.shape, BF16),
            pltpu.VMEM(in_factor.shape, F32),
            pltpu.VMEM(out_factor.shape, F32),
            pltpu.VMEM((tok, rank), BF16),
            pltpu.VMEM((tok, rank), BF16),
            pltpu.VMEM((docs, n, o_rows, rank), BF16),
            pltpu.VMEM((n, docs, o_rows, rank), BF16),
            pltpu.VMEM((o_rows, all_docs, rank), F32),
            pltpu.VMEM((n, all_docs, rows // n), F32),
            pltpu.VMEM((n, all_docs, rows // n), F32),
            pltpu.SemaphoreType.DMA((SLOTS,)),
            pltpu.SemaphoreType.DMA((blocks,)),
            pltpu.SemaphoreType.DMA((4,)),
            pltpu.SemaphoreType.DMA((docs, n)),
            pltpu.SemaphoreType.DMA((n, docs)),
            pltpu.SemaphoreType.DMA((n,)),
            pltpu.SemaphoreType.DMA((n,)),
        ],
        compiler_params=pltpu.CompilerParams(
            collective_id=0, has_side_effects=True, vmem_limit_bytes=52 * 1024 * 1024
        ),
    )(inputs, out_grads, doc_lengths, in_proj, out_proj, in_factor, out_factor, index_rows)
    return scores.T


def general(sizes, inputs, out_grads, doc_lengths, in_proj, out_proj, in_factor, out_factor, index_rows):
    docs, tok, width = inputs.shape
    place = lax.axis_index(("seq", "sub"))
    live = place * tok + jnp.arange(tok, dtype=jnp.int32)[None, :] < doc_lengths[:, None]
    in_rows = jnp.einsum("dtk,kr->dtr", inputs, in_proj, preferred_element_type=F32).astype(BF16)
    out_rows = jnp.einsum("dtk,kr->dtr", out_grads, out_proj, preferred_element_type=F32).astype(BF16)
    out_rows = out_rows * live[:, :, None].astype(BF16)
    grad = jnp.einsum("dto,dti->doi", out_rows, in_rows, preferred_element_type=F32)
    left = jnp.einsum("po,doi->dpi", out_factor, grad, precision=lax.Precision.HIGHEST)
    owned = lax.psum_scatter(left, ("seq", "sub"), scatter_dimension=1, tiled=True)
    precond = jnp.einsum("dpi,iq->dpq", owned, in_factor, precision=lax.Precision.HIGHEST)
    precond = precond.reshape(docs, -1).astype(BF16)
    gathered = lax.all_to_all(precond, "rep", split_axis=1, concat_axis=0, tiled=True)
    scores = jnp.dot(index_rows, gathered.T, preferred_element_type=F32)
    return lax.psum_scatter(scores, OWNERS, scatter_dimension=0, tiled=True)


def on_device(sizes, *arrays):
    inputs, in_proj, index_rows = arrays[0], arrays[3], arrays[7]
    n = sizes[0] * sizes[1] * sizes[2]
    docs, tok, width = inputs.shape
    blocks = n // sizes[2]
    whole = (
        in_proj.shape[1] % (16 * n) == 0
        and index_rows.shape[0] % (128 * n) == 0
        and tok % 32 == 0
        and width % 128 == 0
        and (docs * sizes[2]) % 8 == 0
        and docs >= 2
        and blocks == 2 * PIECES
    )
    return (fused if whole else general)(sizes, *arrays)


def solution(mesh):
    in_specs = (
        P(("grp", "rep"), ("seq", "sub"), None),
        P(("grp", "rep"), ("seq", "sub"), None),
        P(("grp", "rep")),
        P(),
        P(),
        P(),
        P(),
        P("grp", OWNERS),
    )
    sizes = tuple(mesh.shape[axis] for axis in OWNERS)
    return jax.shard_map(
        functools.partial(on_device, sizes),
        mesh=mesh,
        in_specs=in_specs,
        out_specs=P(("grp",) + OWNERS, None),
        check_vma=False,
    )
```

```python
import functools

import jax
import jax.numpy as jnp
from jax import lax
from jax.experimental import pallas as pl
from jax.experimental.pallas import tpu as pltpu
from jax.sharding import PartitionSpec as P

MESH = pl.DeviceIdType.MESH
F32 = jnp.float32
BF16 = jnp.bfloat16
OWNERS = ("seq", "sub", "rep")
PIECES = 4
SLOTS = 8


def two_parts(x):
    high = x.astype(BF16)
    return high, (x - high.astype(F32)).astype(BF16)


def dot3(a, b):
    a_high, a_low = two_parts(a)
    b_high, b_low = two_parts(b)
    small = jnp.dot(a_high, b_low, preferred_element_type=F32) + jnp.dot(
        a_low, b_high, preferred_element_type=F32
    )
    return jnp.dot(a_high, b_high, preferred_element_type=F32) + small


def kernel(
    sizes,
    x_hbm, g_hbm, len_hbm, wi_hbm, wo_hbm, fi_hbm, fo_hbm, idx_hbm,
    out_ref,
    xbuf, idxbuf, wi, wo, fi, fo, lens, held, in_rows, out_rows, turned, send, recv, summed, sc_send, sc_recv,
    piece_sem, idx_sem, weight_sem, send_sem, recv_sem, sc_send_sem, sc_recv_sem,
):
    n_seq, n_sub, n_rep = sizes
    n = n_seq * n_sub * n_rep
    docs, tok, width = x_hbm.shape
    half = width // 2
    blocks = n // n_rep
    rows = idx_hbm.shape[0] // blocks
    lanes = rows // n_rep
    place = lax.axis_index("seq") * n_sub + lax.axis_index("sub")
    my_rep = lax.axis_index("rep")
    me = place * n_rep + my_rep

    def device(p):
        return {
            "seq": lax.div(p, n_sub * n_rep),
            "sub": lax.rem(lax.div(p, n_rep), n_sub),
            "rep": lax.rem(p, n_rep),
        }

    def piece_copy(d, q):
        source = x_hbm if q < 2 else g_hbm
        slot = lax.rem(d, SLOTS // PIECES) * PIECES + q
        return pltpu.make_async_copy(
            source.at[d, :, pl.ds((q % 2) * half, half)], xbuf.at[slot], piece_sem.at[slot]
        )

    def block_at(t):
        return lax.rem(place + 1 + t, blocks)

    def idx_copy(t):
        c = block_at(t)
        return pltpu.make_async_copy(
            idx_hbm.at[pl.ds(c * rows, rows), :], idxbuf.at[t], idx_sem.at[t]
        )

    def weight_copy(k):
        source, target = ((wi_hbm, wi), (wo_hbm, wo), (fo_hbm, fo), (fi_hbm, fi), (len_hbm, lens))[k]
        return pltpu.make_async_copy(source, target, weight_sem.at[k])

    def doc_copy(d, source, p):
        return pltpu.make_async_remote_copy(
            src_ref=send.at[d, p],
            dst_ref=recv.at[source, d],
            send_sem=send_sem.at[d, p],
            recv_sem=recv_sem.at[source, d],
            device_id=device(p),
            device_id_type=MESH,
        )

    def score_copy(source, p):
        return pltpu.make_async_remote_copy(
            src_ref=sc_send.at[p],
            dst_ref=sc_recv.at[source],
            send_sem=sc_send_sem.at[p],
            recv_sem=sc_recv_sem.at[source],
            device_id=device(p),
            device_id_type=MESH,
        )

    weight_copy(0).start()
    piece_copy(0, 0).start()
    piece_copy(0, 1).start()
    weight_copy(1).start()
    piece_copy(0, 2).start()
    piece_copy(0, 3).start()
    weight_copy(2).start()
    weight_copy(3).start()
    weight_copy(4).start()
    for q in range(PIECES):
        piece_copy(1, q).start()

    barrier = pltpu.get_barrier_semaphore()

    def greet(s, carry):
        p = lax.rem(me + s, n)
        pl.semaphore_signal(barrier, inc=1, device_id=device(p), device_id_type=MESH)
        return carry

    lax.fori_loop(1, n, greet, 0)

    def document(d, carry):
        for q in range(PIECES):
            piece_copy(d, q).wait()
            if q % 2 == 0:

                @pl.when(d == 0)
                def _():
                    weight_copy(q // 2).wait()
                    if q == 2:
                        weight_copy(4).wait()

            slot = lax.rem(d, SLOTS // PIECES) * PIECES + q
            w = (wi if q < 2 else wo)[(q % 2) * half : (q % 2 + 1) * half, :]
            product = jnp.dot(xbuf[slot], w, preferred_element_type=F32)
            if q % 2 == 0:
                held[...] = product
            else:
                product = held[...] + product
            if q == 1:
                in_rows[...] = product.astype(BF16)
            elif q == 3:
                position = place * tok + lax.broadcasted_iota(jnp.int32, product.shape, 0)
                out_rows[...] = jnp.where(position < lens[d], product, 0.0).astype(BF16)
            ahead = d + SLOTS // PIECES

            @pl.when(ahead < docs)
            def _():
                piece_copy(ahead, q).start()

            @pl.when(ahead >= docs)
            def _():
                idx_copy((ahead - docs) * PIECES + q).start()

        grad = lax.dot_general(
            out_rows[...], in_rows[...], (((0,), (0,)), ((), ())), preferred_element_type=F32
        )

        @pl.when(d == 0)
        def _():
            weight_copy(2).wait()
            weight_copy(3).wait()

        left = dot3(fo[...], grad)
        send[d] = left.astype(BF16).reshape(send.shape[1:])

        @pl.when(d == 0)
        def _():
            pl.semaphore_wait(barrier, n - 1)

        def push(s, c):
            doc_copy(d, me, lax.rem(me + s, n)).start()
            return c

        lax.fori_loop(1, n, push, 0)
        recv[me, d] = send[d, me]
        return carry

    lax.fori_loop(0, docs, document, 0)

    for d in range(docs):

        def arrive(s, c):
            doc_copy(d, lax.rem(me + n - s, n), lax.rem(me + s, n)).wait_recv()
            return c

        lax.fori_loop(1, n, arrive, 0)
        for r in range(n_rep):
            total = recv[r, d].astype(F32)
            for j in range(1, blocks):
                total = total + recv[j * n_rep + r, d].astype(F32)
            summed[:, r * docs + d, :] = total

    o_rows, all_docs, rank = summed.shape
    columns = o_rows * all_docs
    precond = dot3(summed[...].reshape(columns, rank), fi[...]).T
    column = lax.broadcasted_iota(jnp.int32, precond.shape, 1)
    for o in range(o_rows):
        mine = (column >= o * all_docs) & (column < (o + 1) * all_docs)
        turned[o] = jnp.where(mine, precond, 0.0).astype(BF16)

    def score(u, carry):
        for k in range(n_sub):
            idx_copy(u * n_sub + k).wait()
        part = jnp.dot(
            idxbuf[pl.ds(u * n_sub, n_sub)].reshape(n_sub * rows, o_rows * rank),
            turned[...].reshape(o_rows * rank, columns),
            preferred_element_type=F32,
        ).T
        part = jnp.sum(part.reshape(o_rows, all_docs, n_sub * rows), axis=0)
        for k in range(n_sub):
            c = block_at(u * n_sub + k)
            for r in range(n_rep):
                p = c * n_rep + r
                at = (k * n_rep + r) * lanes
                sc_send[p] = part[:, at : at + lanes]

                @pl.when(p != me)
                def _():
                    score_copy(me, p).start()

        return carry

    lax.fori_loop(0, n_seq, score, 0)
    sc_recv[me] = sc_send[me]

    def settle(s, carry):
        p = lax.rem(me + s, n)
        score_copy(lax.rem(me + n - s, n), p).wait_recv()
        return carry

    lax.fori_loop(1, n, settle, 0)
    out_ref[...] = jnp.sum(sc_recv[...], axis=0)

    def drain(s, carry):
        p = lax.rem(me + s, n)
        score_copy(me, p).wait_send()
        for d in range(docs):
            doc_copy(d, me, p).wait_send()
        return carry

    lax.fori_loop(1, n, drain, 0)


def fused(sizes, inputs, out_grads, doc_lengths, in_proj, out_proj, in_factor, out_factor, index_rows):
    n = sizes[0] * sizes[1] * sizes[2]
    docs, tok, width = inputs.shape
    rank = in_proj.shape[1]
    rows, features = index_rows.shape
    all_docs = docs * sizes[2]
    o_rows = rank // n
    blocks = n // sizes[2]
    in_hbm = pl.BlockSpec(memory_space=pltpu.HBM)
    scores = pl.pallas_call(
        functools.partial(kernel, sizes),
        out_shape=jax.ShapeDtypeStruct((all_docs, rows // n), F32),
        in_specs=[in_hbm] * 8,
        out_specs=pl.BlockSpec(memory_space=pltpu.VMEM),
        scratch_shapes=[
            pltpu.VMEM((SLOTS, tok, width // 2), BF16),
            pltpu.VMEM((blocks, rows // blocks, features), BF16),
            pltpu.VMEM(in_proj.shape, BF16),
            pltpu.VMEM(out_proj.shape, BF16),
            pltpu.VMEM(in_factor.shape, F32),
            pltpu.VMEM(out_factor.shape, F32),
            pltpu.SMEM((docs,), jnp.int32),
            pltpu.VMEM((tok, rank), F32),
            pltpu.VMEM((tok, rank), BF16),
            pltpu.VMEM((tok, rank), BF16),
            pltpu.VMEM((o_rows, rank, o_rows * all_docs), BF16),
            pltpu.VMEM((docs, n, o_rows, rank), BF16),
            pltpu.VMEM((n, docs, o_rows, rank), BF16),
            pltpu.VMEM((o_rows, all_docs, rank), F32),
            pltpu.VMEM((n, all_docs, rows // n), F32),
            pltpu.VMEM((n, all_docs, rows // n), F32),
            pltpu.SemaphoreType.DMA((SLOTS,)),
            pltpu.SemaphoreType.DMA((blocks,)),
            pltpu.SemaphoreType.DMA((5,)),
            pltpu.SemaphoreType.DMA((docs, n)),
            pltpu.SemaphoreType.DMA((n, docs)),
            pltpu.SemaphoreType.DMA((n,)),
            pltpu.SemaphoreType.DMA((n,)),
        ],
        compiler_params=pltpu.CompilerParams(
            collective_id=0, has_side_effects=True, vmem_limit_bytes=52 * 1024 * 1024
        ),
    )(inputs, out_grads, doc_lengths, in_proj, out_proj, in_factor, out_factor, index_rows)
    return scores.T


def general(sizes, inputs, out_grads, doc_lengths, in_proj, out_proj, in_factor, out_factor, index_rows):
    docs, tok, width = inputs.shape
    place = lax.axis_index(("seq", "sub"))
    live = place * tok + jnp.arange(tok, dtype=jnp.int32)[None, :] < doc_lengths[:, None]
    in_rows = jnp.einsum("dtk,kr->dtr", inputs, in_proj, preferred_element_type=F32).astype(BF16)
    out_rows = jnp.einsum("dtk,kr->dtr", out_grads, out_proj, preferred_element_type=F32).astype(BF16)
    out_rows = out_rows * live[:, :, None].astype(BF16)
    grad = jnp.einsum("dto,dti->doi", out_rows, in_rows, preferred_element_type=F32)
    left = jnp.einsum("po,doi->dpi", out_factor, grad, precision=lax.Precision.HIGHEST)
    owned = lax.psum_scatter(left, ("seq", "sub"), scatter_dimension=1, tiled=True)
    precond = jnp.einsum("dpi,iq->dpq", owned, in_factor, precision=lax.Precision.HIGHEST)
    precond = precond.reshape(docs, -1).astype(BF16)
    gathered = lax.all_to_all(precond, "rep", split_axis=1, concat_axis=0, tiled=True)
    scores = jnp.dot(index_rows, gathered.T, preferred_element_type=F32)
    return lax.psum_scatter(scores, OWNERS, scatter_dimension=0, tiled=True)


def on_device(sizes, *arrays):
    inputs, in_proj, index_rows = arrays[0], arrays[3], arrays[7]
    n = sizes[0] * sizes[1] * sizes[2]
    docs, tok, width = inputs.shape
    blocks = n // sizes[2]
    whole = (
        in_proj.shape[1] % (16 * n) == 0
        and index_rows.shape[0] % (128 * n) == 0
        and tok % 16 == 0
        and width % 256 == 0
        and index_rows.shape[1] == in_proj.shape[1] ** 2 // n
        and (docs * sizes[2]) % 8 == 0
        and docs >= 2
        and blocks == 2 * PIECES
    )
    return (fused if whole else general)(sizes, *arrays)


def solution(mesh):
    in_specs = (
        P(("grp", "rep"), ("seq", "sub"), None),
        P(("grp", "rep"), ("seq", "sub"), None),
        P(("grp", "rep")),
        P(),
        P(),
        P(),
        P(),
        P("grp", OWNERS),
    )
    sizes = tuple(mesh.shape[axis] for axis in OWNERS)
    return jax.shard_map(
        functools.partial(on_device, sizes),
        mesh=mesh,
        in_specs=in_specs,
        out_specs=P(("grp",) + OWNERS, None),
        check_vma=False,
    )
```

```python
import functools

import jax
import jax.numpy as jnp
from jax import lax
from jax.experimental import pallas as pl
from jax.experimental.pallas import tpu as pltpu
from jax.sharding import PartitionSpec as P

MESH = pl.DeviceIdType.MESH
F32 = jnp.float32
BF16 = jnp.bfloat16
OWNERS = ("seq", "sub", "rep")
PIECES = 4
SLOTS = 8
CHAINS = 4


def added(parts):
    while len(parts) > 1:
        parts = [a + b for a, b in zip(parts[::2], parts[1::2])]
    return parts[0]


def two_parts(x):
    high = x.astype(BF16)
    return high, (x - high.astype(F32)).astype(BF16)


def dot3(a, b):
    a_high, a_low = two_parts(a)
    b_high, b_low = two_parts(b)
    small = jnp.dot(a_high, b_low, preferred_element_type=F32) + jnp.dot(
        a_low, b_high, preferred_element_type=F32
    )
    return jnp.dot(a_high, b_high, preferred_element_type=F32) + small


def kernel(
    sizes,
    x_hbm, g_hbm, len_hbm, wi_hbm, wo_hbm, fi_hbm, fo_hbm, idx_hbm,
    out_ref,
    xbuf, idxbuf, wi, wo, fi, fo, lens, in_rows, out_rows, turned, send, recv, summed, sc_send, sc_recv,
    piece_sem, idx_sem, weight_sem, send_sem, recv_sem, sc_send_sem, sc_recv_sem,
):
    n_seq, n_sub, n_rep = sizes
    n = n_seq * n_sub * n_rep
    docs, tok, width = x_hbm.shape
    half = width // 2
    step = width // CHAINS
    blocks = n // n_rep
    rows = idx_hbm.shape[0] // blocks
    lanes = rows // n_rep
    place = lax.axis_index("seq") * n_sub + lax.axis_index("sub")
    my_rep = lax.axis_index("rep")
    me = place * n_rep + my_rep

    def device(p):
        return {
            "seq": lax.div(p, n_sub * n_rep),
            "sub": lax.rem(lax.div(p, n_rep), n_sub),
            "rep": lax.rem(p, n_rep),
        }

    def piece_copy(d, q):
        source = x_hbm if q < 2 else g_hbm
        slot = lax.rem(d, SLOTS // PIECES) * PIECES + q
        return pltpu.make_async_copy(
            source.at[d, :, pl.ds((q % 2) * half, half)], xbuf.at[slot], piece_sem.at[slot]
        )

    def block_at(t):
        return lax.rem(place + 1 + t, blocks)

    def idx_copy(t):
        c = block_at(t)
        return pltpu.make_async_copy(
            idx_hbm.at[pl.ds(c * rows, rows), :], idxbuf.at[t], idx_sem.at[t]
        )

    def weight_copy(k):
        source, target = ((wi_hbm, wi), (wo_hbm, wo), (fo_hbm, fo), (fi_hbm, fi), (len_hbm, lens))[k]
        return pltpu.make_async_copy(source, target, weight_sem.at[k])

    def doc_copy(d, source, p):
        return pltpu.make_async_remote_copy(
            src_ref=send.at[d, p],
            dst_ref=recv.at[source, d],
            send_sem=send_sem.at[d, p],
            recv_sem=recv_sem.at[source, d],
            device_id=device(p),
            device_id_type=MESH,
        )

    def score_copy(source, p):
        return pltpu.make_async_remote_copy(
            src_ref=sc_send.at[p],
            dst_ref=sc_recv.at[source],
            send_sem=sc_send_sem.at[p],
            recv_sem=sc_recv_sem.at[source],
            device_id=device(p),
            device_id_type=MESH,
        )

    weight_copy(0).start()
    piece_copy(0, 0).start()
    piece_copy(0, 1).start()
    weight_copy(1).start()
    piece_copy(0, 2).start()
    piece_copy(0, 3).start()
    weight_copy(2).start()
    weight_copy(3).start()
    weight_copy(4).start()
    for q in range(PIECES):
        piece_copy(1, q).start()

    barrier = pltpu.get_barrier_semaphore()

    def greet(s, carry):
        p = lax.rem(me + s, n)
        pl.semaphore_signal(barrier, inc=1, device_id=device(p), device_id_type=MESH)
        return carry

    lax.fori_loop(1, n, greet, 0)

    def document(d, carry):
        first = lax.rem(d, SLOTS // PIECES) * PIECES
        for q in range(0, PIECES, 2):
            piece_copy(d, q).wait()
            piece_copy(d, q + 1).wait()

            @pl.when(d == 0)
            def _():
                weight_copy(q // 2).wait()
                if q == 2:
                    weight_copy(4).wait()

            w = wi if q == 0 else wo
            chains = []
            for k in range(CHAINS):
                h, at = (k * 2) // CHAINS, (k % (CHAINS // 2)) * step
                chains.append(
                    jnp.dot(
                        xbuf[first + q + h, :, at : at + step],
                        w[k * step : (k + 1) * step, :],
                        preferred_element_type=F32,
                    )
                )
            product = added(chains)
            if q == 0:
                in_rows[...] = product.astype(BF16)
            else:
                position = place * tok + lax.broadcasted_iota(jnp.int32, product.shape, 0)
                out_rows[...] = jnp.where(position < lens[d], product, 0.0).astype(BF16)
            ahead = d + SLOTS // PIECES
            for k in (q, q + 1):

                @pl.when(ahead < docs)
                def _():
                    piece_copy(ahead, k).start()

                @pl.when(ahead >= docs)
                def _():
                    idx_copy((ahead - docs) * PIECES + k).start()

        grad = lax.dot_general(
            out_rows[...], in_rows[...], (((0,), (0,)), ((), ())), preferred_element_type=F32
        )

        @pl.when(d == 0)
        def _():
            weight_copy(2).wait()
            weight_copy(3).wait()

        left = dot3(fo[...], grad)
        send[d] = left.astype(BF16).reshape(send.shape[1:])

        @pl.when(d == 0)
        def _():
            pl.semaphore_wait(barrier, n - 1)

        def push(s, c):
            doc_copy(d, me, lax.rem(me + s, n)).start()
            return c

        lax.fori_loop(1, n, push, 0)
        recv[me, d] = send[d, me]
        return carry

    lax.fori_loop(0, docs, document, 0)

    for d in range(docs):

        def arrive(s, c):
            doc_copy(d, lax.rem(me + n - s, n), lax.rem(me + s, n)).wait_recv()
            return c

        lax.fori_loop(1, n, arrive, 0)
        for r in range(n_rep):
            total = recv[r, d].astype(F32)
            for j in range(1, blocks):
                total = total + recv[j * n_rep + r, d].astype(F32)
            summed[:, r * docs + d, :] = total

    o_rows, all_docs, rank = summed.shape
    columns = o_rows * all_docs
    precond = dot3(summed[...].reshape(columns, rank), fi[...]).T
    column = lax.broadcasted_iota(jnp.int32, precond.shape, 1)
    for o in range(o_rows):
        mine = (column >= o * all_docs) & (column < (o + 1) * all_docs)
        turned[o] = jnp.where(mine, precond, 0.0).astype(BF16)

    def score(u, carry):
        for k in range(n_sub):
            idx_copy(u * n_sub + k).wait()
        parts = []
        for k in range(CHAINS):
            o, wide = k * (o_rows // CHAINS), o_rows // CHAINS
            block = idxbuf[pl.ds(u * n_sub, n_sub), :, o * rank : (o + wide) * rank]
            parts.append(
                jnp.dot(
                    block.reshape(n_sub * rows, wide * rank),
                    turned[o : o + wide].reshape(wide * rank, columns),
                    preferred_element_type=F32,
                )
            )
        part = added(parts).T
        part = jnp.sum(part.reshape(o_rows, all_docs, n_sub * rows), axis=0)
        for k in range(n_sub):
            c = block_at(u * n_sub + k)
            for r in range(n_rep):
                p = c * n_rep + r
                at = (k * n_rep + r) * lanes
                sc_send[p] = part[:, at : at + lanes]

                @pl.when(p != me)
                def _():
                    score_copy(me, p).start()

        return carry

    lax.fori_loop(0, n_seq, score, 0)
    sc_recv[me] = sc_send[me]

    def settle(s, carry):
        p = lax.rem(me + s, n)
        score_copy(lax.rem(me + n - s, n), p).wait_recv()
        return carry

    lax.fori_loop(1, n, settle, 0)
    out_ref[...] = jnp.sum(sc_recv[...], axis=0)

    def drain(s, carry):
        p = lax.rem(me + s, n)
        score_copy(me, p).wait_send()
        for d in range(docs):
            doc_copy(d, me, p).wait_send()
        return carry

    lax.fori_loop(1, n, drain, 0)


def fused(sizes, inputs, out_grads, doc_lengths, in_proj, out_proj, in_factor, out_factor, index_rows):
    n = sizes[0] * sizes[1] * sizes[2]
    docs, tok, width = inputs.shape
    rank = in_proj.shape[1]
    rows, features = index_rows.shape
    all_docs = docs * sizes[2]
    o_rows = rank // n
    blocks = n // sizes[2]
    in_hbm = pl.BlockSpec(memory_space=pltpu.HBM)
    scores = pl.pallas_call(
        functools.partial(kernel, sizes),
        out_shape=jax.ShapeDtypeStruct((all_docs, rows // n), F32),
        in_specs=[in_hbm] * 8,
        out_specs=pl.BlockSpec(memory_space=pltpu.VMEM),
        scratch_shapes=[
            pltpu.VMEM((SLOTS, tok, width // 2), BF16),
            pltpu.VMEM((blocks, rows // blocks, features), BF16),
            pltpu.VMEM(in_proj.shape, BF16),
            pltpu.VMEM(out_proj.shape, BF16),
            pltpu.VMEM(in_factor.shape, F32),
            pltpu.VMEM(out_factor.shape, F32),
            pltpu.SMEM((docs,), jnp.int32),
            pltpu.VMEM((tok, rank), BF16),
            pltpu.VMEM((tok, rank), BF16),
            pltpu.VMEM((o_rows, rank, o_rows * all_docs), BF16),
            pltpu.VMEM((docs, n, o_rows, rank), BF16),
            pltpu.VMEM((n, docs, o_rows, rank), BF16),
            pltpu.VMEM((o_rows, all_docs, rank), F32),
            pltpu.VMEM((n, all_docs, rows // n), F32),
            pltpu.VMEM((n, all_docs, rows // n), F32),
            pltpu.SemaphoreType.DMA((SLOTS,)),
            pltpu.SemaphoreType.DMA((blocks,)),
            pltpu.SemaphoreType.DMA((5,)),
            pltpu.SemaphoreType.DMA((docs, n)),
            pltpu.SemaphoreType.DMA((n, docs)),
            pltpu.SemaphoreType.DMA((n,)),
            pltpu.SemaphoreType.DMA((n,)),
        ],
        compiler_params=pltpu.CompilerParams(
            collective_id=0, has_side_effects=True, vmem_limit_bytes=64 * 1024 * 1024
        ),
    )(inputs, out_grads, doc_lengths, in_proj, out_proj, in_factor, out_factor, index_rows)
    return scores.T


def general(sizes, inputs, out_grads, doc_lengths, in_proj, out_proj, in_factor, out_factor, index_rows):
    docs, tok, width = inputs.shape
    place = lax.axis_index(("seq", "sub"))
    live = place * tok + jnp.arange(tok, dtype=jnp.int32)[None, :] < doc_lengths[:, None]
    in_rows = jnp.einsum("dtk,kr->dtr", inputs, in_proj, preferred_element_type=F32).astype(BF16)
    out_rows = jnp.einsum("dtk,kr->dtr", out_grads, out_proj, preferred_element_type=F32).astype(BF16)
    out_rows = out_rows * live[:, :, None].astype(BF16)
    grad = jnp.einsum("dto,dti->doi", out_rows, in_rows, preferred_element_type=F32)
    left = jnp.einsum("po,doi->dpi", out_factor, grad, precision=lax.Precision.HIGHEST)
    owned = lax.psum_scatter(left, ("seq", "sub"), scatter_dimension=1, tiled=True)
    precond = jnp.einsum("dpi,iq->dpq", owned, in_factor, precision=lax.Precision.HIGHEST)
    precond = precond.reshape(docs, -1).astype(BF16)
    gathered = lax.all_to_all(precond, "rep", split_axis=1, concat_axis=0, tiled=True)
    scores = jnp.dot(index_rows, gathered.T, preferred_element_type=F32)
    return lax.psum_scatter(scores, OWNERS, scatter_dimension=0, tiled=True)


def on_device(sizes, *arrays):
    inputs, in_proj, index_rows = arrays[0], arrays[3], arrays[7]
    n = sizes[0] * sizes[1] * sizes[2]
    docs, tok, width = inputs.shape
    blocks = n // sizes[2]
    whole = (
        in_proj.shape[1] % (16 * n) == 0
        and index_rows.shape[0] % (128 * n) == 0
        and tok % 16 == 0
        and width % (128 * CHAINS) == 0
        and index_rows.shape[1] == in_proj.shape[1] ** 2 // n
        and (docs * sizes[2]) % 8 == 0
        and docs >= 2
        and blocks == 2 * PIECES
    )
    return (fused if whole else general)(sizes, *arrays)


def solution(mesh):
    in_specs = (
        P(("grp", "rep"), ("seq", "sub"), None),
        P(("grp", "rep"), ("seq", "sub"), None),
        P(("grp", "rep")),
        P(),
        P(),
        P(),
        P(),
        P("grp", OWNERS),
    )
    sizes = tuple(mesh.shape[axis] for axis in OWNERS)
    return jax.shard_map(
        functools.partial(on_device, sizes),
        mesh=mesh,
        in_specs=in_specs,
        out_specs=P(("grp",) + OWNERS, None),
        check_vma=False,
    )
```

```python
import functools

import jax
import jax.numpy as jnp
from jax import lax
from jax.experimental import pallas as pl
from jax.experimental.pallas import tpu as pltpu
from jax.sharding import PartitionSpec as P

MESH = pl.DeviceIdType.MESH
F32 = jnp.float32
BF16 = jnp.bfloat16
OWNERS = ("seq", "sub", "rep")
PIECES = 4
SLOTS = 8
CHAINS = 4


def added(parts):
    while len(parts) > 1:
        parts = [a + b for a, b in zip(parts[::2], parts[1::2])]
    return parts[0]


def two_parts(x):
    high = x.astype(BF16)
    return high, (x - high.astype(F32)).astype(BF16)


def dot3(a, b):
    a_high, a_low = two_parts(a)
    b_high, b_low = two_parts(b)
    small = jnp.dot(a_high, b_low, preferred_element_type=F32) + jnp.dot(
        a_low, b_high, preferred_element_type=F32
    )
    return jnp.dot(a_high, b_high, preferred_element_type=F32) + small


def kernel(
    sizes,
    x_hbm, g_hbm, len_hbm, wi_hbm, wo_hbm, fi_hbm, fo_hbm, idx_hbm,
    out_ref,
    xbuf, idxbuf, wi, wo, fi, fo, lens, in_rows, out_rows, turned, part_sums, pair_send, pair_recv, send, recv, summed, sc_send, sc_recv,
    piece_sem, idx_sem, weight_sem, pair_send_sem, pair_recv_sem, send_sem, recv_sem, sc_send_sem, sc_recv_sem,
):
    n_seq, n_sub, n_rep = sizes
    n = n_seq * n_sub * n_rep
    docs, tok, width = x_hbm.shape
    half = width // 2
    step = width // CHAINS
    blocks = n // n_rep
    rows = idx_hbm.shape[0] // blocks
    lanes = rows // n_rep
    my_seq, my_sub, my_rep = (lax.axis_index(axis) for axis in OWNERS)
    place = my_seq * n_sub + my_sub
    column = n_seq * n_rep
    mine = my_seq * n_rep + my_rep
    me = place * n_rep + my_rep

    def device(p):
        return {
            "seq": lax.div(p, n_sub * n_rep),
            "sub": lax.rem(lax.div(p, n_rep), n_sub),
            "rep": lax.rem(p, n_rep),
        }

    def piece_copy(d, q):
        source = x_hbm if q < 2 else g_hbm
        slot = lax.rem(d, SLOTS // PIECES) * PIECES + q
        return pltpu.make_async_copy(
            source.at[d, :, pl.ds((q % 2) * half, half)], xbuf.at[slot], piece_sem.at[slot]
        )

    def block_at(t):
        return lax.rem(place + 1 + t, blocks)

    def idx_copy(t):
        c = block_at(t)
        return pltpu.make_async_copy(
            idx_hbm.at[pl.ds(c * rows, rows), :], idxbuf.at[t], idx_sem.at[t]
        )

    def weight_copy(k):
        source, target = ((wi_hbm, wi), (wo_hbm, wo), (fo_hbm, fo), (fi_hbm, fi), (len_hbm, lens))[k]
        return pltpu.make_async_copy(source, target, weight_sem.at[k])

    def pair_copy(d, k):
        to = lax.rem(my_sub + k, n_sub)
        return pltpu.make_async_remote_copy(
            src_ref=pair_send.at[d, to],
            dst_ref=pair_recv.at[d, k - 1],
            send_sem=pair_send_sem.at[d, k - 1],
            recv_sem=pair_recv_sem.at[d, k - 1],
            device_id={"seq": my_seq, "sub": to, "rep": my_rep},
            device_id_type=MESH,
        )

    def doc_copy(d, source, v):
        return pltpu.make_async_remote_copy(
            src_ref=send.at[d, v],
            dst_ref=recv.at[source, d],
            send_sem=send_sem.at[d, v],
            recv_sem=recv_sem.at[source, d],
            device_id={"seq": lax.div(v, n_rep), "sub": my_sub, "rep": lax.rem(v, n_rep)},
            device_id_type=MESH,
        )

    def pass_on(d):
        total = part_sums[my_sub]
        for k in range(1, n_sub):
            pair_copy(d, k).wait_recv()
            total = total + pair_recv[d, k - 1].astype(F32)
        send[d] = total.astype(BF16).reshape(send.shape[1:])

        def push(s, c):
            doc_copy(d, mine, lax.rem(mine + s, column)).start()
            return c

        lax.fori_loop(1, column, push, 0)
        recv[mine, d] = send[d, mine]

    def score_copy(source, p):
        return pltpu.make_async_remote_copy(
            src_ref=sc_send.at[p],
            dst_ref=sc_recv.at[source],
            send_sem=sc_send_sem.at[p],
            recv_sem=sc_recv_sem.at[source],
            device_id=device(p),
            device_id_type=MESH,
        )

    weight_copy(0).start()
    piece_copy(0, 0).start()
    piece_copy(0, 1).start()
    weight_copy(1).start()
    piece_copy(0, 2).start()
    piece_copy(0, 3).start()
    weight_copy(2).start()
    weight_copy(3).start()
    weight_copy(4).start()
    for q in range(PIECES):
        piece_copy(1, q).start()

    barrier = pltpu.get_barrier_semaphore()

    def greet(s, carry):
        p = lax.rem(me + s, n)
        pl.semaphore_signal(barrier, inc=1, device_id=device(p), device_id_type=MESH)
        return carry

    lax.fori_loop(1, n, greet, 0)

    def document(d, carry):
        first = lax.rem(d, SLOTS // PIECES) * PIECES
        for q in range(0, PIECES, 2):
            piece_copy(d, q).wait()
            piece_copy(d, q + 1).wait()

            @pl.when(d == 0)
            def _():
                weight_copy(q // 2).wait()
                if q == 2:
                    weight_copy(4).wait()

            w = wi if q == 0 else wo
            chains = []
            for k in range(CHAINS):
                h, at = (k * 2) // CHAINS, (k % (CHAINS // 2)) * step
                chains.append(
                    jnp.dot(
                        xbuf[first + q + h, :, at : at + step],
                        w[k * step : (k + 1) * step, :],
                        preferred_element_type=F32,
                    )
                )
            product = added(chains)
            if q == 0:
                in_rows[...] = product.astype(BF16)

                @pl.when(d == 0)
                def _():
                    pl.semaphore_wait(barrier, n - 1)

                @pl.when(d > 0)
                def _():
                    pass_on(d - 1)

            else:
                position = place * tok + lax.broadcasted_iota(jnp.int32, product.shape, 0)
                out_rows[...] = jnp.where(position < lens[d], product, 0.0).astype(BF16)
            ahead = d + SLOTS // PIECES
            for k in (q, q + 1):

                @pl.when(ahead < docs)
                def _():
                    piece_copy(ahead, k).start()

                @pl.when(ahead >= docs)
                def _():
                    idx_copy((ahead - docs) * PIECES + k).start()

        grad = lax.dot_general(
            out_rows[...], in_rows[...], (((0,), (0,)), ((), ())), preferred_element_type=F32
        )

        @pl.when(d == 0)
        def _():
            weight_copy(2).wait()
            weight_copy(3).wait()

        left = dot3(fo[...], grad).reshape(n_seq, n_sub, -1, grad.shape[1])
        for k in range(n_sub):
            part_sums[k] = left[:, k]
            pair_send[d, k] = left[:, k].astype(BF16)

        for k in range(1, n_sub):
            pair_copy(d, k).start()
        return carry

    lax.fori_loop(0, docs, document, 0)
    pass_on(docs - 1)

    for d in range(docs):

        def arrive(s, c):
            doc_copy(d, lax.rem(mine + column - s, column), lax.rem(mine + s, column)).wait_recv()
            return c

        lax.fori_loop(1, column, arrive, 0)
        for r in range(n_rep):
            total = recv[r, d].astype(F32)
            for j in range(1, n_seq):
                total = total + recv[j * n_rep + r, d].astype(F32)
            summed[:, r * docs + d, :] = total

    o_rows, all_docs, rank = summed.shape
    columns = o_rows * all_docs
    precond = dot3(summed[...].reshape(columns, rank), fi[...]).T
    lane = lax.broadcasted_iota(jnp.int32, precond.shape, 1)
    for o in range(o_rows):
        kept = (lane >= o * all_docs) & (lane < (o + 1) * all_docs)
        turned[o] = jnp.where(kept, precond, 0.0).astype(BF16)

    def score(u, carry):
        for k in range(n_sub):
            idx_copy(u * n_sub + k).wait()
        parts = []
        for k in range(CHAINS):
            o, wide = k * (o_rows // CHAINS), o_rows // CHAINS
            block = idxbuf[pl.ds(u * n_sub, n_sub), :, o * rank : (o + wide) * rank]
            parts.append(
                jnp.dot(
                    block.reshape(n_sub * rows, wide * rank),
                    turned[o : o + wide].reshape(wide * rank, columns),
                    preferred_element_type=F32,
                )
            )
        part = added(parts).T
        part = jnp.sum(part.reshape(o_rows, all_docs, n_sub * rows), axis=0)
        for k in range(n_sub):
            c = block_at(u * n_sub + k)
            for r in range(n_rep):
                p = c * n_rep + r
                at = (k * n_rep + r) * lanes
                sc_send[p] = part[:, at : at + lanes]

                @pl.when(p != me)
                def _():
                    score_copy(me, p).start()

        return carry

    lax.fori_loop(0, n_seq, score, 0)
    sc_recv[me] = sc_send[me]

    def settle(s, carry):
        p = lax.rem(me + s, n)
        score_copy(lax.rem(me + n - s, n), p).wait_recv()
        return carry

    lax.fori_loop(1, n, settle, 0)
    out_ref[...] = jnp.sum(sc_recv[...], axis=0)

    def drain(s, carry):
        score_copy(me, lax.rem(me + s, n)).wait_send()
        return carry

    lax.fori_loop(1, n, drain, 0)

    def drain_docs(d, carry):
        for k in range(1, n_sub):
            pair_copy(d, k).wait_send()
        for s in range(1, column):
            doc_copy(d, mine, lax.rem(mine + s, column)).wait_send()
        return carry

    lax.fori_loop(0, docs, drain_docs, 0)


def fused(sizes, inputs, out_grads, doc_lengths, in_proj, out_proj, in_factor, out_factor, index_rows):
    n_seq, n_sub, n_rep = sizes
    n = n_seq * n_sub * n_rep
    docs, tok, width = inputs.shape
    rank = in_proj.shape[1]
    rows, features = index_rows.shape
    all_docs = docs * sizes[2]
    o_rows = rank // n
    blocks = n // sizes[2]
    in_hbm = pl.BlockSpec(memory_space=pltpu.HBM)
    scores = pl.pallas_call(
        functools.partial(kernel, sizes),
        out_shape=jax.ShapeDtypeStruct((all_docs, rows // n), F32),
        in_specs=[in_hbm] * 8,
        out_specs=pl.BlockSpec(memory_space=pltpu.VMEM),
        scratch_shapes=[
            pltpu.VMEM((SLOTS, tok, width // 2), BF16),
            pltpu.VMEM((blocks, rows // blocks, features), BF16),
            pltpu.VMEM(in_proj.shape, BF16),
            pltpu.VMEM(out_proj.shape, BF16),
            pltpu.VMEM(in_factor.shape, F32),
            pltpu.VMEM(out_factor.shape, F32),
            pltpu.SMEM((docs,), jnp.int32),
            pltpu.VMEM((tok, rank), BF16),
            pltpu.VMEM((tok, rank), BF16),
            pltpu.VMEM((o_rows, rank, o_rows * all_docs), BF16),
            pltpu.VMEM((n_sub, n_seq, n_rep * o_rows, rank), F32),
            pltpu.VMEM((docs, n_sub, n_seq, n_rep * o_rows, rank), BF16),
            pltpu.VMEM((docs, n_sub - 1, n_seq, n_rep * o_rows, rank), BF16),
            pltpu.VMEM((docs, n_seq * n_rep, o_rows, rank), BF16),
            pltpu.VMEM((n_seq * n_rep, docs, o_rows, rank), BF16),
            pltpu.VMEM((o_rows, all_docs, rank), F32),
            pltpu.VMEM((n, all_docs, rows // n), F32),
            pltpu.VMEM((n, all_docs, rows // n), F32),
            pltpu.SemaphoreType.DMA((SLOTS,)),
            pltpu.SemaphoreType.DMA((blocks,)),
            pltpu.SemaphoreType.DMA((5,)),
            pltpu.SemaphoreType.DMA((docs, n_sub - 1)),
            pltpu.SemaphoreType.DMA((docs, n_sub - 1)),
            pltpu.SemaphoreType.DMA((docs, n_seq * n_rep)),
            pltpu.SemaphoreType.DMA((n_seq * n_rep, docs)),
            pltpu.SemaphoreType.DMA((n,)),
            pltpu.SemaphoreType.DMA((n,)),
        ],
        compiler_params=pltpu.CompilerParams(
            collective_id=0, has_side_effects=True, vmem_limit_bytes=64 * 1024 * 1024
        ),
    )(inputs, out_grads, doc_lengths, in_proj, out_proj, in_factor, out_factor, index_rows)
    return scores.T


def general(sizes, inputs, out_grads, doc_lengths, in_proj, out_proj, in_factor, out_factor, index_rows):
    docs, tok, width = inputs.shape
    place = lax.axis_index(("seq", "sub"))
    live = place * tok + jnp.arange(tok, dtype=jnp.int32)[None, :] < doc_lengths[:, None]
    in_rows = jnp.einsum("dtk,kr->dtr", inputs, in_proj, preferred_element_type=F32).astype(BF16)
    out_rows = jnp.einsum("dtk,kr->dtr", out_grads, out_proj, preferred_element_type=F32).astype(BF16)
    out_rows = out_rows * live[:, :, None].astype(BF16)
    grad = jnp.einsum("dto,dti->doi", out_rows, in_rows, preferred_element_type=F32)
    left = jnp.einsum("po,doi->dpi", out_factor, grad, precision=lax.Precision.HIGHEST)
    owned = lax.psum_scatter(left, ("seq", "sub"), scatter_dimension=1, tiled=True)
    precond = jnp.einsum("dpi,iq->dpq", owned, in_factor, precision=lax.Precision.HIGHEST)
    precond = precond.reshape(docs, -1).astype(BF16)
    gathered = lax.all_to_all(precond, "rep", split_axis=1, concat_axis=0, tiled=True)
    scores = jnp.dot(index_rows, gathered.T, preferred_element_type=F32)
    return lax.psum_scatter(scores, OWNERS, scatter_dimension=0, tiled=True)


def on_device(sizes, *arrays):
    inputs, in_proj, index_rows = arrays[0], arrays[3], arrays[7]
    n = sizes[0] * sizes[1] * sizes[2]
    docs, tok, width = inputs.shape
    blocks = n // sizes[2]
    whole = (
        in_proj.shape[1] % (16 * n) == 0
        and index_rows.shape[0] % (128 * n) == 0
        and tok % 16 == 0
        and width % (128 * CHAINS) == 0
        and index_rows.shape[1] == in_proj.shape[1] ** 2 // n
        and (docs * sizes[2]) % 8 == 0
        and docs >= 2
        and sizes[1] >= 2
        and blocks == 2 * PIECES
    )
    return (fused if whole else general)(sizes, *arrays)


def solution(mesh):
    in_specs = (
        P(("grp", "rep"), ("seq", "sub"), None),
        P(("grp", "rep"), ("seq", "sub"), None),
        P(("grp", "rep")),
        P(),
        P(),
        P(),
        P(),
        P("grp", OWNERS),
    )
    sizes = tuple(mesh.shape[axis] for axis in OWNERS)
    return jax.shard_map(
        functools.partial(on_device, sizes),
        mesh=mesh,
        in_specs=in_specs,
        out_specs=P(("grp",) + OWNERS, None),
        check_vma=False,
    )
```

```python
import functools

import jax
import jax.numpy as jnp
from jax import lax
from jax.experimental import pallas as pl
from jax.experimental.pallas import tpu as pltpu
from jax.sharding import PartitionSpec as P

MESH = pl.DeviceIdType.MESH
F32 = jnp.float32
BF16 = jnp.bfloat16
OWNERS = ("seq", "sub", "rep")
PIECES = 4
SLOTS = 8
CHAINS = 4


def added(parts):
    while len(parts) > 1:
        parts = [a + b for a, b in zip(parts[::2], parts[1::2])]
    return parts[0]


def two_parts(x):
    high = x.astype(BF16)
    return high, (x - high.astype(F32)).astype(BF16)


def dot3(a, b):
    a_high, a_low = two_parts(a)
    b_high, b_low = two_parts(b)
    small = jnp.dot(a_high, b_low, preferred_element_type=F32) + jnp.dot(
        a_low, b_high, preferred_element_type=F32
    )
    return jnp.dot(a_high, b_high, preferred_element_type=F32) + small


def kernel(
    sizes,
    x_hbm, g_hbm, len_hbm, wi_hbm, wo_hbm, fi_hbm, fo_hbm, idx_hbm,
    out_ref,
    xbuf, idxbuf, wi, wo, fi, fo, lens, held, in_rows, out_rows, turned, send, recv, summed, sc_send, sc_recv,
    piece_sem, idx_sem, weight_sem, send_sem, recv_sem, sc_send_sem, sc_recv_sem,
):
    n_seq, n_sub, n_rep = sizes
    n = n_seq * n_sub * n_rep
    docs, tok, width = x_hbm.shape
    half = width // 2
    step = width // CHAINS
    blocks = n // n_rep
    rows = idx_hbm.shape[0] // blocks
    lanes = rows // n_rep
    my_seq, my_sub, my_rep = (lax.axis_index(axis) for axis in OWNERS)
    place = my_seq * n_sub + my_sub
    me = place * n_rep + my_rep

    def others():
        for shift in range(1, n):
            seq = lax.rem(my_seq + shift // (n_sub * n_rep), n_seq)
            sub = lax.rem(my_sub + shift // n_rep % n_sub, n_sub)
            rep = lax.rem(my_rep + shift % n_rep, n_rep)
            yield {"seq": seq, "sub": sub, "rep": rep}, (seq * n_sub + sub) * n_rep + rep

    def piece_copy(d, q):
        source = x_hbm if q < 2 else g_hbm
        slot = lax.rem(d, SLOTS // PIECES) * PIECES + q
        return pltpu.make_async_copy(
            source.at[d, :, pl.ds((q % 2) * half, half)], xbuf.at[slot], piece_sem.at[slot]
        )

    def block_at(t):
        return lax.rem(place + 1 + t, blocks)

    def idx_copy(t):
        c = block_at(t)
        return pltpu.make_async_copy(
            idx_hbm.at[pl.ds(c * rows, rows), :], idxbuf.at[t], idx_sem.at[t]
        )

    def weight_copy(k):
        halves = pl.ds(0, half), pl.ds(half, half)
        source, target = (
            (wi_hbm.at[halves[0], :], wi.at[halves[0], :]),
            (wi_hbm.at[halves[1], :], wi.at[halves[1], :]),
            (wo_hbm.at[halves[0], :], wo.at[halves[0], :]),
            (wo_hbm.at[halves[1], :], wo.at[halves[1], :]),
            (len_hbm, lens),
            (fo_hbm, fo),
            (fi_hbm, fi),
        )[k]
        return pltpu.make_async_copy(source, target, weight_sem.at[k])

    def doc_copy(d, source, p, target, count=None):
        at = (lambda k: k) if count is None else (lambda k: pl.ds(k, count))
        return pltpu.make_async_remote_copy(
            src_ref=send.at[d, at(p)],
            dst_ref=recv.at[d, at(source)],
            send_sem=send_sem.at[d],
            recv_sem=recv_sem.at[d],
            device_id=target,
            device_id_type=MESH,
        )

    def score_copy(source, p, target, count=None):
        at = (lambda k: k) if count is None else (lambda k: pl.ds(k, count))
        return pltpu.make_async_remote_copy(
            src_ref=sc_send.at[at(p)],
            dst_ref=sc_recv.at[at(source)],
            send_sem=sc_send_sem,
            recv_sem=sc_recv_sem,
            device_id=target,
            device_id_type=MESH,
        )

    next_device = next(others())[0]

    for q in range(PIECES):
        weight_copy(q).start()
        piece_copy(0, q).start()
    for k in range(PIECES, 7):
        weight_copy(k).start()

    barrier = pltpu.get_barrier_semaphore()

    for target, _ in others():
        pl.semaphore_signal(barrier, inc=1, device_id=target, device_id_type=MESH)

    def document(d, carry):
        first = lax.rem(d, SLOTS // PIECES) * PIECES
        for q in range(PIECES):
            piece_copy(d, q).wait()

            @pl.when(d == 0)
            def _():
                weight_copy(q).wait()

            @pl.when(d + 1 < docs)
            def _():
                piece_copy(d + 1, q).start()

            @pl.when(d + 1 == docs)
            def _():
                idx_copy(q).start()
                idx_copy(PIECES + q).start()

            w = wi if q < 2 else wo
            chains = []
            for k in range(CHAINS // 2):
                row = (q % 2) * half + k * step
                chains.append(
                    jnp.dot(
                        xbuf[first + q, :, k * step : (k + 1) * step],
                        w[row : row + step, :],
                        preferred_element_type=F32,
                    )
                )
            product = added(chains)
            if q % 2 == 0:
                held[...] = product
            else:
                product = held[...] + product
            if q == 1:
                in_rows[...] = product.astype(BF16)
            elif q == 3:

                @pl.when(d == 0)
                def _():
                    weight_copy(4).wait()

                position = place * tok + lax.broadcasted_iota(jnp.int32, product.shape, 0)
                out_rows[...] = jnp.where(position < lens[d], product, 0.0).astype(BF16)

        grad = lax.dot_general(
            out_rows[...], in_rows[...], (((0,), (0,)), ((), ())), preferred_element_type=F32
        )

        @pl.when(d == 0)
        def _():
            weight_copy(5).wait()
            weight_copy(6).wait()

        left = dot3(fo[...], grad)
        send[d] = left.astype(BF16).reshape(send.shape[1:])

        @pl.when(d == 0)
        def _():
            pl.semaphore_wait(barrier, n - 1)

        for target, p in others():
            doc_copy(d, me, p, target).start()
        recv[d, me] = send[d, me]
        return carry

    lax.fori_loop(0, docs, document, 0)

    for d in range(docs):
        doc_copy(d, 0, 0, next_device, n - 1).wait_recv()
        for r in range(n_rep):
            total = recv[d, r].astype(F32)
            for j in range(1, blocks):
                total = total + recv[d, j * n_rep + r].astype(F32)
            summed[:, r * docs + d, :] = total

    o_rows, all_docs, rank = summed.shape
    columns = o_rows * all_docs
    precond = dot3(summed[...].reshape(columns, rank), fi[...]).T
    column = lax.broadcasted_iota(jnp.int32, precond.shape, 1)
    for o in range(o_rows):
        mine = (column >= o * all_docs) & (column < (o + 1) * all_docs)
        turned[o] = jnp.where(mine, precond, 0.0).astype(BF16)

    def score(u, carry):
        for k in range(n_sub):
            idx_copy(u * n_sub + k).wait()
        parts = []
        for k in range(CHAINS):
            o, wide = k * (o_rows // CHAINS), o_rows // CHAINS
            block = idxbuf[pl.ds(u * n_sub, n_sub), :, o * rank : (o + wide) * rank]
            parts.append(
                jnp.dot(
                    block.reshape(n_sub * rows, wide * rank),
                    turned[o : o + wide].reshape(wide * rank, columns),
                    preferred_element_type=F32,
                )
            )
        part = added(parts).T
        part = jnp.sum(part.reshape(o_rows, all_docs, n_sub * rows), axis=0)
        for k in range(n_sub):
            c = block_at(u * n_sub + k)
            for r in range(n_rep):
                p = c * n_rep + r
                at = (k * n_rep + r) * lanes
                sc_send[p] = part[:, at : at + lanes]

                @pl.when(p != me)
                def _():
                    target = {"seq": lax.div(c, n_sub), "sub": lax.rem(c, n_sub), "rep": r}
                    score_copy(me, p, target).start()

        return carry

    lax.fori_loop(0, n_seq, score, 0)
    sc_recv[me] = sc_send[me]

    score_copy(0, 0, next_device, n - 1).wait_recv()
    out_ref[...] = jnp.sum(sc_recv[...], axis=0)
    score_copy(0, 0, next_device, n - 1).wait_send()
    for d in range(docs):
        doc_copy(d, 0, 0, next_device, n - 1).wait_send()


def fused(sizes, inputs, out_grads, doc_lengths, in_proj, out_proj, in_factor, out_factor, index_rows):
    n = sizes[0] * sizes[1] * sizes[2]
    docs, tok, width = inputs.shape
    rank = in_proj.shape[1]
    rows, features = index_rows.shape
    all_docs = docs * sizes[2]
    o_rows = rank // n
    blocks = n // sizes[2]
    in_hbm = pl.BlockSpec(memory_space=pltpu.HBM)
    scores = pl.pallas_call(
        functools.partial(kernel, sizes),
        out_shape=jax.ShapeDtypeStruct((all_docs, rows // n), F32),
        in_specs=[in_hbm] * 8,
        out_specs=pl.BlockSpec(memory_space=pltpu.VMEM),
        scratch_shapes=[
            pltpu.VMEM((SLOTS, tok, width // 2), BF16),
            pltpu.VMEM((blocks, rows // blocks, features), BF16),
            pltpu.VMEM(in_proj.shape, BF16),
            pltpu.VMEM(out_proj.shape, BF16),
            pltpu.VMEM(in_factor.shape, F32),
            pltpu.VMEM(out_factor.shape, F32),
            pltpu.SMEM((docs,), jnp.int32),
            pltpu.VMEM((tok, rank), F32),
            pltpu.VMEM((tok, rank), BF16),
            pltpu.VMEM((tok, rank), BF16),
            pltpu.VMEM((o_rows, rank, o_rows * all_docs), BF16),
            pltpu.VMEM((docs, n, o_rows, rank), BF16),
            pltpu.VMEM((docs, n, o_rows, rank), BF16),
            pltpu.VMEM((o_rows, all_docs, rank), F32),
            pltpu.VMEM((n, all_docs, rows // n), F32),
            pltpu.VMEM((n, all_docs, rows // n), F32),
            pltpu.SemaphoreType.DMA((SLOTS,)),
            pltpu.SemaphoreType.DMA((blocks,)),
            pltpu.SemaphoreType.DMA((7,)),
            pltpu.SemaphoreType.DMA((docs,)),
            pltpu.SemaphoreType.DMA((docs,)),
            pltpu.SemaphoreType.DMA,
            pltpu.SemaphoreType.DMA,
        ],
        compiler_params=pltpu.CompilerParams(
            collective_id=0, has_side_effects=True, vmem_limit_bytes=64 * 1024 * 1024
        ),
    )(inputs, out_grads, doc_lengths, in_proj, out_proj, in_factor, out_factor, index_rows)
    return scores.T


def general(sizes, inputs, out_grads, doc_lengths, in_proj, out_proj, in_factor, out_factor, index_rows):
    docs, tok, width = inputs.shape
    place = lax.axis_index(("seq", "sub"))
    live = place * tok + jnp.arange(tok, dtype=jnp.int32)[None, :] < doc_lengths[:, None]
    in_rows = jnp.einsum("dtk,kr->dtr", inputs, in_proj, preferred_element_type=F32).astype(BF16)
    out_rows = jnp.einsum("dtk,kr->dtr", out_grads, out_proj, preferred_element_type=F32).astype(BF16)
    out_rows = out_rows * live[:, :, None].astype(BF16)
    grad = jnp.einsum("dto,dti->doi", out_rows, in_rows, preferred_element_type=F32)
    left = jnp.einsum("po,doi->dpi", out_factor, grad, precision=lax.Precision.HIGHEST)
    owned = lax.psum_scatter(left, ("seq", "sub"), scatter_dimension=1, tiled=True)
    precond = jnp.einsum("dpi,iq->dpq", owned, in_factor, precision=lax.Precision.HIGHEST)
    precond = precond.reshape(docs, -1).astype(BF16)
    gathered = lax.all_to_all(precond, "rep", split_axis=1, concat_axis=0, tiled=True)
    scores = jnp.dot(index_rows, gathered.T, preferred_element_type=F32)
    return lax.psum_scatter(scores, OWNERS, scatter_dimension=0, tiled=True)


def on_device(sizes, *arrays):
    inputs, in_proj, index_rows = arrays[0], arrays[3], arrays[7]
    n = sizes[0] * sizes[1] * sizes[2]
    docs, tok, width = inputs.shape
    blocks = n // sizes[2]
    whole = (
        in_proj.shape[1] % (16 * n) == 0
        and index_rows.shape[0] % (128 * n) == 0
        and tok % 16 == 0
        and width % (128 * CHAINS) == 0
        and index_rows.shape[1] == in_proj.shape[1] ** 2 // n
        and (docs * sizes[2]) % 8 == 0
        and docs >= 2
        and blocks == 2 * PIECES
    )
    return (fused if whole else general)(sizes, *arrays)


def solution(mesh):
    in_specs = (
        P(("grp", "rep"), ("seq", "sub"), None),
        P(("grp", "rep"), ("seq", "sub"), None),
        P(("grp", "rep")),
        P(),
        P(),
        P(),
        P(),
        P("grp", OWNERS),
    )
    sizes = tuple(mesh.shape[axis] for axis in OWNERS)
    return jax.shard_map(
        functools.partial(on_device, sizes),
        mesh=mesh,
        in_specs=in_specs,
        out_specs=P(("grp",) + OWNERS, None),
        check_vma=False,
    )
```

```python
import functools

import jax
import jax.numpy as jnp
from jax import lax
from jax.experimental import pallas as pl
from jax.experimental.pallas import tpu as pltpu
from jax.sharding import PartitionSpec as P

MESH = pl.DeviceIdType.MESH
F32 = jnp.float32
BF16 = jnp.bfloat16
OWNERS = ("seq", "sub", "rep")
PIECES = 4
SLOTS = 8
CHAINS = 4


def added(parts):
    while len(parts) > 1:
        parts = [a + b for a, b in zip(parts[::2], parts[1::2])]
    return parts[0]


def two_parts(x):
    high = x.astype(BF16)
    return high, (x - high.astype(F32)).astype(BF16)


def dot3(a, b):
    a_high, a_low = two_parts(a)
    b_high, b_low = two_parts(b)
    small = jnp.dot(a_high, b_low, preferred_element_type=F32) + jnp.dot(
        a_low, b_high, preferred_element_type=F32
    )
    return jnp.dot(a_high, b_high, preferred_element_type=F32) + small


def kernel(
    sizes,
    x_hbm, g_hbm, len_hbm, wi_hbm, wo_hbm, fi_hbm, fo_hbm, idx_hbm,
    out_ref,
    xbuf, idxbuf, wi, wo, fi, fo, lens, held, in_rows, out_rows, turned, send, recv, summed, sc_send, sc_recv,
    piece_sem, idx_sem, weight_sem, send_sem, recv_sem, sc_send_sem, sc_recv_sem,
):
    n_seq, n_sub, n_rep = sizes
    n = n_seq * n_sub * n_rep
    docs, tok, width = x_hbm.shape
    half = width // 2
    step = width // CHAINS
    blocks = n // n_rep
    rows = idx_hbm.shape[0] // blocks
    lanes = rows // n_rep
    my_seq, my_sub, my_rep = (lax.axis_index(axis) for axis in OWNERS)
    place = my_seq * n_sub + my_sub
    me = place * n_rep + my_rep

    def others():
        for shift in range(1, n):
            seq = lax.rem(my_seq + shift // (n_sub * n_rep), n_seq)
            sub = lax.rem(my_sub + shift // n_rep % n_sub, n_sub)
            rep = lax.rem(my_rep + shift % n_rep, n_rep)
            yield {"seq": seq, "sub": sub, "rep": rep}, (seq * n_sub + sub) * n_rep + rep

    def piece_copy(d, q):
        source = x_hbm if q < 2 else g_hbm
        slot = lax.rem(d, SLOTS // PIECES) * PIECES + q
        return pltpu.make_async_copy(
            source.at[d, :, pl.ds((q % 2) * half, half)], xbuf.at[slot], piece_sem.at[slot]
        )

    def block_at(t):
        return lax.rem(place + 1 + t, blocks)

    def idx_copy(t):
        c = block_at(t)
        return pltpu.make_async_copy(
            idx_hbm.at[pl.ds(c * rows, rows), :], idxbuf.at[t], idx_sem.at[t]
        )

    def weight_copy(k):
        halves = pl.ds(0, half), pl.ds(half, half)
        source, target = (
            (wi_hbm.at[halves[0], :], wi.at[halves[0], :]),
            (wi_hbm.at[halves[1], :], wi.at[halves[1], :]),
            (wo_hbm.at[halves[0], :], wo.at[halves[0], :]),
            (wo_hbm.at[halves[1], :], wo.at[halves[1], :]),
            (len_hbm, lens),
            (fo_hbm, fo),
            (fi_hbm, fi),
        )[k]
        return pltpu.make_async_copy(source, target, weight_sem.at[k])

    def doc_copy(d, source, p, target, count=None):
        at = (lambda k: k) if count is None else (lambda k: pl.ds(k, count))
        return pltpu.make_async_remote_copy(
            src_ref=send.at[d, at(p)],
            dst_ref=recv.at[d, at(source)],
            send_sem=send_sem.at[d],
            recv_sem=recv_sem.at[d],
            device_id=target,
            device_id_type=MESH,
        )

    def score_copy(source, p, target, count=None):
        at = (lambda k: k) if count is None else (lambda k: pl.ds(k, count))
        return pltpu.make_async_remote_copy(
            src_ref=sc_send.at[at(p)],
            dst_ref=sc_recv.at[at(source)],
            send_sem=sc_send_sem,
            recv_sem=sc_recv_sem,
            device_id=target,
            device_id_type=MESH,
        )

    next_device = next(others())[0]

    for q in range(PIECES):
        weight_copy(q).start()
        piece_copy(0, q).start()
    for k in range(PIECES, 7):
        weight_copy(k).start()

    barrier = pltpu.get_barrier_semaphore()

    for target, _ in others():
        pl.semaphore_signal(barrier, inc=1, device_id=target, device_id_type=MESH)

    def document(d, carry):
        first = lax.rem(d, SLOTS // PIECES) * PIECES
        for q in range(PIECES):
            piece_copy(d, q).wait()

            @pl.when(d == 0)
            def _():
                weight_copy(q).wait()

            @pl.when(d + 1 < docs)
            def _():
                piece_copy(d + 1, q).start()

            @pl.when(d + 1 == docs)
            def _():
                idx_copy(2 * q).start()
                idx_copy(2 * q + 1).start()

            w = wi if q < 2 else wo
            chains = []
            for k in range(CHAINS // 2):
                row = (q % 2) * half + k * step
                chains.append(
                    jnp.dot(
                        xbuf[first + q, :, k * step : (k + 1) * step],
                        w[row : row + step, :],
                        preferred_element_type=F32,
                    )
                )
            product = added(chains)
            if q % 2 == 0:
                held[...] = product
            else:
                product = held[...] + product
            if q == 1:
                in_rows[...] = product.astype(BF16)
            elif q == 3:

                @pl.when(d == 0)
                def _():
                    weight_copy(4).wait()

                position = place * tok + lax.broadcasted_iota(jnp.int32, product.shape, 0)
                out_rows[...] = jnp.where(position < lens[d], product, 0.0).astype(BF16)

        grad = lax.dot_general(
            out_rows[...], in_rows[...], (((0,), (0,)), ((), ())), preferred_element_type=F32
        )

        @pl.when(d == 0)
        def _():
            weight_copy(5).wait()
            weight_copy(6).wait()

        left = dot3(fo[...], grad)
        send[d] = left.astype(BF16).reshape(send.shape[1:])

        @pl.when(d == 0)
        def _():
            pl.semaphore_wait(barrier, n - 1)

        for target, p in others():
            doc_copy(d, me, p, target).start()
        recv[d, me] = send[d, me]
        return carry

    lax.fori_loop(0, docs, document, 0)

    for d in range(docs):
        doc_copy(d, 0, 0, next_device, n - 1).wait_recv()
        for r in range(n_rep):
            total = recv[d, r].astype(F32)
            for j in range(1, blocks):
                total = total + recv[d, j * n_rep + r].astype(F32)
            summed[:, r * docs + d, :] = total

    o_rows, all_docs, rank = summed.shape
    columns = o_rows * all_docs
    precond = dot3(summed[...].reshape(columns, rank), fi[...]).T
    column = lax.broadcasted_iota(jnp.int32, precond.shape, 1)
    for o in range(o_rows):
        mine = (column >= o * all_docs) & (column < (o + 1) * all_docs)
        turned[o] = jnp.where(mine, precond, 0.0).astype(BF16)

    def products(u):
        for k in range(n_sub):
            idx_copy(u * n_sub + k).wait()
        parts = []
        for k in range(CHAINS):
            o, wide = k * (o_rows // CHAINS), o_rows // CHAINS
            block = idxbuf[u * n_sub : (u + 1) * n_sub, :, o * rank : (o + wide) * rank]
            parts.append(
                jnp.dot(
                    block.reshape(n_sub * rows, wide * rank),
                    turned[o : o + wide].reshape(wide * rank, columns),
                    preferred_element_type=F32,
                )
            )
        return added(parts)

    def hand_out(u, part):
        part = jnp.sum(part.T.reshape(o_rows, all_docs, n_sub * rows), axis=0)
        for k in range(n_sub):
            t = u * n_sub + k
            c = block_at(t)
            for r in range(n_rep):
                at = (k * n_rep + r) * lanes
                sc_send[c * n_rep + r] = part[:, at : at + lanes]
            for r in range(n_rep):
                p = c * n_rep + r
                copy = score_copy(
                    me, p, {"seq": lax.div(c, n_sub), "sub": lax.rem(c, n_sub), "rep": r}
                )
                if t < blocks - 1:
                    copy.start()
                else:
                    pl.when(r != my_rep)(copy.start)

    part = products(0)
    for u in range(1, n_seq):
        later = products(u)
        hand_out(u - 1, part)
        part = later
    hand_out(n_seq - 1, part)
    sc_recv[me] = sc_send[me]

    score_copy(0, 0, next_device, n - 1).wait_recv()
    out_ref[...] = jnp.sum(sc_recv[...], axis=0)
    score_copy(0, 0, next_device, n - 1).wait_send()
    for d in range(docs):
        doc_copy(d, 0, 0, next_device, n - 1).wait_send()


def fused(sizes, inputs, out_grads, doc_lengths, in_proj, out_proj, in_factor, out_factor, index_rows):
    n = sizes[0] * sizes[1] * sizes[2]
    docs, tok, width = inputs.shape
    rank = in_proj.shape[1]
    rows, features = index_rows.shape
    all_docs = docs * sizes[2]
    o_rows = rank // n
    blocks = n // sizes[2]
    in_hbm = pl.BlockSpec(memory_space=pltpu.HBM)
    scores = pl.pallas_call(
        functools.partial(kernel, sizes),
        out_shape=jax.ShapeDtypeStruct((all_docs, rows // n), F32),
        in_specs=[in_hbm] * 8,
        out_specs=pl.BlockSpec(memory_space=pltpu.VMEM),
        scratch_shapes=[
            pltpu.VMEM((SLOTS, tok, width // 2), BF16),
            pltpu.VMEM((blocks, rows // blocks, features), BF16),
            pltpu.VMEM(in_proj.shape, BF16),
            pltpu.VMEM(out_proj.shape, BF16),
            pltpu.VMEM(in_factor.shape, F32),
            pltpu.VMEM(out_factor.shape, F32),
            pltpu.SMEM((docs,), jnp.int32),
            pltpu.VMEM((tok, rank), F32),
            pltpu.VMEM((tok, rank), BF16),
            pltpu.VMEM((tok, rank), BF16),
            pltpu.VMEM((o_rows, rank, o_rows * all_docs), BF16),
            pltpu.VMEM((docs, n, o_rows, rank), BF16),
            pltpu.VMEM((docs, n, o_rows, rank), BF16),
            pltpu.VMEM((o_rows, all_docs, rank), F32),
            pltpu.VMEM((n, all_docs, rows // n), F32),
            pltpu.VMEM((n, all_docs, rows // n), F32),
            pltpu.SemaphoreType.DMA((SLOTS,)),
            pltpu.SemaphoreType.DMA((blocks,)),
            pltpu.SemaphoreType.DMA((7,)),
            pltpu.SemaphoreType.DMA((docs,)),
            pltpu.SemaphoreType.DMA((docs,)),
            pltpu.SemaphoreType.DMA,
            pltpu.SemaphoreType.DMA,
        ],
        compiler_params=pltpu.CompilerParams(
            collective_id=0, has_side_effects=True, vmem_limit_bytes=64 * 1024 * 1024
        ),
    )(inputs, out_grads, doc_lengths, in_proj, out_proj, in_factor, out_factor, index_rows)
    return scores.T


def general(sizes, inputs, out_grads, doc_lengths, in_proj, out_proj, in_factor, out_factor, index_rows):
    docs, tok, width = inputs.shape
    place = lax.axis_index(("seq", "sub"))
    live = place * tok + jnp.arange(tok, dtype=jnp.int32)[None, :] < doc_lengths[:, None]
    in_rows = jnp.einsum("dtk,kr->dtr", inputs, in_proj, preferred_element_type=F32).astype(BF16)
    out_rows = jnp.einsum("dtk,kr->dtr", out_grads, out_proj, preferred_element_type=F32).astype(BF16)
    out_rows = out_rows * live[:, :, None].astype(BF16)
    grad = jnp.einsum("dto,dti->doi", out_rows, in_rows, preferred_element_type=F32)
    left = jnp.einsum("po,doi->dpi", out_factor, grad, precision=lax.Precision.HIGHEST)
    owned = lax.psum_scatter(left, ("seq", "sub"), scatter_dimension=1, tiled=True)
    precond = jnp.einsum("dpi,iq->dpq", owned, in_factor, precision=lax.Precision.HIGHEST)
    precond = precond.reshape(docs, -1).astype(BF16)
    gathered = lax.all_to_all(precond, "rep", split_axis=1, concat_axis=0, tiled=True)
    scores = jnp.dot(index_rows, gathered.T, preferred_element_type=F32)
    return lax.psum_scatter(scores, OWNERS, scatter_dimension=0, tiled=True)


def on_device(sizes, *arrays):
    inputs, in_proj, index_rows = arrays[0], arrays[3], arrays[7]
    n = sizes[0] * sizes[1] * sizes[2]
    docs, tok, width = inputs.shape
    blocks = n // sizes[2]
    whole = (
        in_proj.shape[1] % (16 * n) == 0
        and index_rows.shape[0] % (128 * n) == 0
        and tok % 16 == 0
        and width % (128 * CHAINS) == 0
        and index_rows.shape[1] == in_proj.shape[1] ** 2 // n
        and (docs * sizes[2]) % 8 == 0
        and docs >= 2
        and blocks == 2 * PIECES
    )
    return (fused if whole else general)(sizes, *arrays)


def solution(mesh):
    in_specs = (
        P(("grp", "rep"), ("seq", "sub"), None),
        P(("grp", "rep"), ("seq", "sub"), None),
        P(("grp", "rep")),
        P(),
        P(),
        P(),
        P(),
        P("grp", OWNERS),
    )
    sizes = tuple(mesh.shape[axis] for axis in OWNERS)
    return jax.shard_map(
        functools.partial(on_device, sizes),
        mesh=mesh,
        in_specs=in_specs,
        out_specs=P(("grp",) + OWNERS, None),
        check_vma=False,
    )
```

```python
import functools

import jax
import jax.numpy as jnp
from jax import lax
from jax.experimental import pallas as pl
from jax.experimental.pallas import tpu as pltpu
from jax.sharding import PartitionSpec as P

MESH = pl.DeviceIdType.MESH
F32 = jnp.float32
BF16 = jnp.bfloat16
OWNERS = ("seq", "sub", "rep")
PIECES = 4
SLOTS = 8
CHAINS = 4


def added(parts):
    while len(parts) > 1:
        parts = [a + b for a, b in zip(parts[::2], parts[1::2])]
    return parts[0]


def two_parts(x):
    high = x.astype(BF16)
    return high, (x - high.astype(F32)).astype(BF16)


def dot3(a, b):
    a_high, a_low = two_parts(a)
    b_high, b_low = two_parts(b)
    small = jnp.dot(a_high, b_low, preferred_element_type=F32) + jnp.dot(
        a_low, b_high, preferred_element_type=F32
    )
    return jnp.dot(a_high, b_high, preferred_element_type=F32) + small


def kernel(
    sizes,
    x_hbm, g_hbm, len_hbm, wi_hbm, wo_hbm, fi_hbm, fo_hbm, idx_hbm,
    out_ref,
    xbuf, idxbuf, weights, fi, fo, lens, held, in_rows, out_rows, turned, send, recv, summed, sc_send, sc_recv,
    piece_sem, idx_sem, weight_sem, send_sem, recv_sem, sc_send_sem, sc_recv_sem,
):
    n_seq, n_sub, n_rep = sizes
    n = n_seq * n_sub * n_rep
    docs, tok, width = x_hbm.shape
    half = width // 2
    step = width // CHAINS
    blocks = n // n_rep
    rows = idx_hbm.shape[0] // blocks
    lanes = rows // n_rep
    my_seq, my_sub, my_rep = (lax.axis_index(axis) for axis in OWNERS)
    place = my_seq * n_sub + my_sub
    me = place * n_rep + my_rep

    def others():
        for shift in range(1, n):
            seq = lax.rem(my_seq + shift // (n_sub * n_rep), n_seq)
            sub = lax.rem(my_sub + shift // n_rep % n_sub, n_sub)
            rep = lax.rem(my_rep + shift % n_rep, n_rep)
            yield {"seq": seq, "sub": sub, "rep": rep}, (seq * n_sub + sub) * n_rep + rep

    def piece_copy(d, q):
        source = x_hbm if q < 2 else g_hbm
        slot = lax.rem(d, SLOTS // PIECES) * PIECES + q
        return pltpu.make_async_copy(
            source.at[d, :, pl.ds((q % 2) * half, half)], xbuf.at[slot], piece_sem.at[slot]
        )

    def block_at(t):
        return lax.rem(place + 1 + t, blocks)

    def idx_copy(t):
        c = block_at(t)
        return pltpu.make_async_copy(
            idx_hbm.at[pl.ds(c * rows, rows), :], idxbuf.at[t], idx_sem.at[t]
        )

    def weight_copy(k):
        halves = pl.ds(0, half), pl.ds(half, half)
        source, target = (
            (wi_hbm.at[halves[0], :], weights.at[0]),
            (wi_hbm.at[halves[1], :], weights.at[1]),
            (wo_hbm.at[halves[0], :], weights.at[2]),
            (wo_hbm.at[halves[1], :], weights.at[3]),
            (len_hbm, lens),
            (fo_hbm, fo),
            (fi_hbm, fi),
        )[k]
        return pltpu.make_async_copy(source, target, weight_sem.at[k])

    def doc_copy(d, source, p, target, count=None):
        at = (lambda k: k) if count is None else (lambda k: pl.ds(k, count))
        return pltpu.make_async_remote_copy(
            src_ref=send.at[d, at(p)],
            dst_ref=recv.at[d, at(source)],
            send_sem=send_sem.at[d],
            recv_sem=recv_sem.at[d],
            device_id=target,
            device_id_type=MESH,
        )

    def score_copy(source, p, target, count=None):
        at = (lambda k: k) if count is None else (lambda k: pl.ds(k, count))
        return pltpu.make_async_remote_copy(
            src_ref=sc_send.at[at(p)],
            dst_ref=sc_recv.at[at(source)],
            send_sem=sc_send_sem,
            recv_sem=sc_recv_sem,
            device_id=target,
            device_id_type=MESH,
        )

    next_device = next(others())[0]

    for q in range(PIECES):
        weight_copy(q).start()
        piece_copy(0, q).start()
    for k in range(PIECES, 7):
        weight_copy(k).start()

    barrier = pltpu.get_barrier_semaphore()

    for target, _ in others():
        pl.semaphore_signal(barrier, inc=1, device_id=target, device_id_type=MESH)

    def document(d, carry):
        first = lax.rem(d, SLOTS // PIECES) * PIECES
        def piece(q, c):
            slot = first + q
            pltpu.make_async_copy(
                x_hbm.at[d, :, pl.ds(0, half)], xbuf.at[slot], piece_sem.at[slot]
            ).wait()

            @pl.when(d == 0)
            def _():
                pltpu.make_async_copy(
                    wi_hbm.at[pl.ds(0, half), :], weights.at[q], weight_sem.at[q]
                ).wait()

            for k in range(PIECES):

                @pl.when((d + 1 < docs) & (q == k))
                def _():
                    piece_copy(d + 1, k).start()

            @pl.when(d + 1 == docs)
            def _():
                idx_copy(2 * q).start()
                idx_copy(2 * q + 1).start()

            chains = []
            for k in range(CHAINS // 2):
                chains.append(
                    jnp.dot(
                        xbuf[slot, :, k * step : (k + 1) * step],
                        weights[q, k * step : (k + 1) * step, :],
                        preferred_element_type=F32,
                    )
                )
            product = added(chains)
            side = lax.div(q, 2)

            @pl.when(lax.rem(q, 2) == 0)
            def _():
                held[side] = product

            @pl.when(lax.rem(q, 2) == 1)
            def _():
                held[side] = held[side] + product

            return c

        lax.fori_loop(0, PIECES, piece, 0)

        @pl.when(d == 0)
        def _():
            weight_copy(4).wait()

        in_rows[...] = held[0].astype(BF16)
        position = place * tok + lax.broadcasted_iota(jnp.int32, (tok, held.shape[2]), 0)
        out_rows[...] = jnp.where(position < lens[d], held[1], 0.0).astype(BF16)
        grad = lax.dot_general(
            out_rows[...], in_rows[...], (((0,), (0,)), ((), ())), preferred_element_type=F32
        )

        @pl.when(d == 0)
        def _():
            weight_copy(5).wait()
            weight_copy(6).wait()

        left = dot3(fo[...], grad)
        send[d] = left.astype(BF16).reshape(send.shape[1:])

        @pl.when(d == 0)
        def _():
            pl.semaphore_wait(barrier, n - 1)

        for target, p in others():
            doc_copy(d, me, p, target).start()
        recv[d, me] = send[d, me]
        return carry

    lax.fori_loop(0, docs, document, 0)

    for d in range(docs):
        doc_copy(d, 0, 0, next_device, n - 1).wait_recv()
        for r in range(n_rep):
            total = recv[d, r].astype(F32)
            for j in range(1, blocks):
                total = total + recv[d, j * n_rep + r].astype(F32)
            summed[:, r * docs + d, :] = total

    o_rows, all_docs, rank = summed.shape
    columns = o_rows * all_docs
    precond = dot3(summed[...].reshape(columns, rank), fi[...]).T
    column = lax.broadcasted_iota(jnp.int32, precond.shape, 1)
    for o in range(o_rows):
        mine = (column >= o * all_docs) & (column < (o + 1) * all_docs)
        turned[o] = jnp.where(mine, precond, 0.0).astype(BF16)

    def score(u, carry):
        for k in range(n_sub):
            idx_copy(u * n_sub + k).wait()
        parts = []
        for k in range(CHAINS):
            o, wide = k * (o_rows // CHAINS), o_rows // CHAINS
            block = idxbuf[pl.ds(u * n_sub, n_sub), :, o * rank : (o + wide) * rank]
            parts.append(
                jnp.dot(
                    block.reshape(n_sub * rows, wide * rank),
                    turned[o : o + wide].reshape(wide * rank, columns),
                    preferred_element_type=F32,
                )
            )
        part = added(parts).T
        part = jnp.sum(part.reshape(o_rows, all_docs, n_sub * rows), axis=0)
        for k in range(n_sub):
            c = block_at(u * n_sub + k)
            for r in range(n_rep):
                p = c * n_rep + r
                at = (k * n_rep + r) * lanes
                sc_send[p] = part[:, at : at + lanes]

                @pl.when(p != me)
                def _():
                    target = {"seq": lax.div(c, n_sub), "sub": lax.rem(c, n_sub), "rep": r}
                    score_copy(me, p, target).start()

        return carry

    lax.fori_loop(0, n_seq, score, 0)
    sc_recv[me] = sc_send[me]

    score_copy(0, 0, next_device, n - 1).wait_recv()
    out_ref[...] = jnp.sum(sc_recv[...], axis=0)
    score_copy(0, 0, next_device, n - 1).wait_send()
    for d in range(docs):
        doc_copy(d, 0, 0, next_device, n - 1).wait_send()


def fused(sizes, inputs, out_grads, doc_lengths, in_proj, out_proj, in_factor, out_factor, index_rows):
    n = sizes[0] * sizes[1] * sizes[2]
    docs, tok, width = inputs.shape
    rank = in_proj.shape[1]
    rows, features = index_rows.shape
    all_docs = docs * sizes[2]
    o_rows = rank // n
    blocks = n // sizes[2]
    in_hbm = pl.BlockSpec(memory_space=pltpu.HBM)
    scores = pl.pallas_call(
        functools.partial(kernel, sizes),
        out_shape=jax.ShapeDtypeStruct((all_docs, rows // n), F32),
        in_specs=[in_hbm] * 8,
        out_specs=pl.BlockSpec(memory_space=pltpu.VMEM),
        scratch_shapes=[
            pltpu.VMEM((SLOTS, tok, width // 2), BF16),
            pltpu.VMEM((blocks, rows // blocks, features), BF16),
            pltpu.VMEM((PIECES, width // 2, rank), BF16),
            pltpu.VMEM(in_factor.shape, F32),
            pltpu.VMEM(out_factor.shape, F32),
            pltpu.SMEM((docs,), jnp.int32),
            pltpu.VMEM((2, tok, rank), F32),
            pltpu.VMEM((tok, rank), BF16),
            pltpu.VMEM((tok, rank), BF16),
            pltpu.VMEM((o_rows, rank, o_rows * all_docs), BF16),
            pltpu.VMEM((docs, n, o_rows, rank), BF16),
            pltpu.VMEM((docs, n, o_rows, rank), BF16),
            pltpu.VMEM((o_rows, all_docs, rank), F32),
            pltpu.VMEM((n, all_docs, rows // n), F32),
            pltpu.VMEM((n, all_docs, rows // n), F32),
            pltpu.SemaphoreType.DMA((SLOTS,)),
            pltpu.SemaphoreType.DMA((blocks,)),
            pltpu.SemaphoreType.DMA((7,)),
            pltpu.SemaphoreType.DMA((docs,)),
            pltpu.SemaphoreType.DMA((docs,)),
            pltpu.SemaphoreType.DMA,
            pltpu.SemaphoreType.DMA,
        ],
        compiler_params=pltpu.CompilerParams(
            collective_id=0, has_side_effects=True, vmem_limit_bytes=64 * 1024 * 1024
        ),
    )(inputs, out_grads, doc_lengths, in_proj, out_proj, in_factor, out_factor, index_rows)
    return scores.T


def general(sizes, inputs, out_grads, doc_lengths, in_proj, out_proj, in_factor, out_factor, index_rows):
    docs, tok, width = inputs.shape
    place = lax.axis_index(("seq", "sub"))
    live = place * tok + jnp.arange(tok, dtype=jnp.int32)[None, :] < doc_lengths[:, None]
    in_rows = jnp.einsum("dtk,kr->dtr", inputs, in_proj, preferred_element_type=F32).astype(BF16)
    out_rows = jnp.einsum("dtk,kr->dtr", out_grads, out_proj, preferred_element_type=F32).astype(BF16)
    out_rows = out_rows * live[:, :, None].astype(BF16)
    grad = jnp.einsum("dto,dti->doi", out_rows, in_rows, preferred_element_type=F32)
    left = jnp.einsum("po,doi->dpi", out_factor, grad, precision=lax.Precision.HIGHEST)
    owned = lax.psum_scatter(left, ("seq", "sub"), scatter_dimension=1, tiled=True)
    precond = jnp.einsum("dpi,iq->dpq", owned, in_factor, precision=lax.Precision.HIGHEST)
    precond = precond.reshape(docs, -1).astype(BF16)
    gathered = lax.all_to_all(precond, "rep", split_axis=1, concat_axis=0, tiled=True)
    scores = jnp.dot(index_rows, gathered.T, preferred_element_type=F32)
    return lax.psum_scatter(scores, OWNERS, scatter_dimension=0, tiled=True)


def on_device(sizes, *arrays):
    inputs, in_proj, index_rows = arrays[0], arrays[3], arrays[7]
    n = sizes[0] * sizes[1] * sizes[2]
    docs, tok, width = inputs.shape
    blocks = n // sizes[2]
    whole = (
        in_proj.shape[1] % (16 * n) == 0
        and index_rows.shape[0] % (128 * n) == 0
        and tok % 16 == 0
        and width % (128 * CHAINS) == 0
        and index_rows.shape[1] == in_proj.shape[1] ** 2 // n
        and (docs * sizes[2]) % 8 == 0
        and docs >= 2
        and blocks == 2 * PIECES
    )
    return (fused if whole else general)(sizes, *arrays)


def solution(mesh):
    in_specs = (
        P(("grp", "rep"), ("seq", "sub"), None),
        P(("grp", "rep"), ("seq", "sub"), None),
        P(("grp", "rep")),
        P(),
        P(),
        P(),
        P(),
        P("grp", OWNERS),
    )
    sizes = tuple(mesh.shape[axis] for axis in OWNERS)
    return jax.shard_map(
        functools.partial(on_device, sizes),
        mesh=mesh,
        in_specs=in_specs,
        out_specs=P(("grp",) + OWNERS, None),
        check_vma=False,
    )
```
